512 devices in a mesh: dp: 128 (over y, z, core), rep: 4 (over x).
Axes of the slice: x: 4, y: 8, z: 8, core: 2. Of those that a mesh axis runs over, the one named last changes fastest.
Arguments:
- tokens: bfloat16 [262144, 512], P(('dp', 'rep')), may hold values from -6 to 6
- owner_cotangent: bfloat16 [393216, 512], P(('dp', 'rep')), may hold values from -6 to 6
- proj_weight: bfloat16 [512, 2048], replicated, may hold values from -0.25 to 0.25
- out_weight: bfloat16 [512, 512], replicated, may hold values from -0.25 to 0.25
- bias_table: float32 [4, 10], replicated, may hold values from -1 to 1
- history_length: int32 [2048], P(('dp', 'rep')), may hold values from 1 to 512, as said below
- first_block: int32 [2048], P(('dp', 'rep')), may hold values from 0 to 3, as said below
- owner_slot: int32 [2048], P(('dp', 'rep')), may hold values from 0 to 3071, as said below
Outputs:
- token_grad: bfloat16 [262144, 512], P(('dp', 'rep'))
- proj_grad: float32 [512, 2048], P(None, ('dp', 'rep'))
- out_grad: float32 [512, 512], replicated
- bias_grad: float32 [4, 10], replicated
The draws below stay inside these ranges and needn't reach their ends.
Inputs may be any that keep to these rules, and one draw needn't show every extreme that they name: `history_length`: A history of n blocks occupies n consecutive blocks of one aligned group of 4 blocks and has between (n - 1) * 128 + 1 and n * 128 tokens; all its blocks carry its length. `first_block`: all blocks of a history carry the offset, within their group of 4, of the history's first block. owner_slot = o * 6 + s. The owner o of a block on device (dp index d, rep index e) is the device (d + r mod 128, e), 0 <= r < 2, the same r for all blocks of a history; histories of more than 2 blocks have r = 0. Slots 0 to 3 of an owner take blocks of its own device; slots 4 + (r - 1) * 2 onward take at most 2 blocks of the device r steps back along dp. A history's blocks take consecutive slots in order; no slot takes two blocks. In every draw some device sends 2 blocks at a nonzero offset.
All inputs are finite; a program needn't handle non-finite values.
Results may differ from the reference program's by a relative error of at most 0.011.
Values may be sent and summed in bfloat16 or wider, within the bound.
A program may use at most 128 MiB of HBM per device.

```python
import jax
import jax.numpy as jnp
import numpy as np
from jax import lax

HEADS = 4
HEAD_DIM = 128
D = 512
BLOCK = 128
BLK_DEV = 4
REACH = 2
CAP = 2
BUCKETS = 10
TOKENS = 262144
OWN_ROWS = 393216
N_DP = 128
N_REP = 4


def routing(key):
    loader_count = N_DP * N_REP
    key_breaks, key_forced, key_tails, key_prefs = jax.random.split(key, 4)
    column = jnp.arange(BLK_DEV, dtype=jnp.int32)[None, :]
    loader_ids = jnp.arange(loader_count, dtype=jnp.int32)[:, None]
    reach_index = jnp.arange(REACH, dtype=jnp.int32)[None, :]
    top_loader = (N_DP - 1) * N_REP - 1
    forced = (top_loader + 1 + jax.random.randint(key_forced, (), 0, loader_count - 3)) % loader_count
    forced = jnp.where(forced == 0, top_loader + 1, forced).astype(jnp.int32)
    full_loader = (forced + 1) % loader_count
    last_loader = (forced + 2) % loader_count
    is_forced = loader_ids == forced
    is_top = loader_ids == top_loader
    is_full = loader_ids == full_loader
    is_last = loader_ids == last_loader
    breaks = jax.random.randint(key_breaks, (loader_count, BLK_DEV), 0, 2).astype(jnp.int32)
    breaks = jnp.where(is_full, 0, breaks)
    breaks = jnp.where(is_last, 1, breaks)
    forced_row = jnp.where(column == 1, 0, 1).astype(jnp.int32)
    breaks = jnp.where(is_forced | is_top, forced_row, breaks)
    breaks = jnp.where(column == 0, 1, breaks)
    tails = jax.random.randint(key_tails, (loader_count, BLK_DEV), 1, BLOCK + 1).astype(jnp.int32)
    tails = jnp.where(is_full & (column == 0), BLOCK, tails)
    prefs = jax.random.randint(key_prefs, (loader_count, BLK_DEV), 0, REACH).astype(jnp.int32)
    prefs = jnp.where((loader_ids == 0) & (column == 0), 0, prefs)
    prefs = jnp.where((is_forced | is_top) & (column == 0), 1, prefs)
    firsts = []
    for block_index in range(BLK_DEV):
        earlier = firsts[-1] if block_index > 0 else jnp.zeros((loader_count,), jnp.int32)
        firsts.append(jnp.where(breaks[:, block_index] == 1, block_index, earlier).astype(jnp.int32))
    first = jnp.stack(firsts, axis=1)
    blocks_in = jnp.sum((first[:, :, None] == first[:, None, :]).astype(jnp.int32), axis=-1)
    tail_at = jnp.take_along_axis(tails, first, axis=1)
    lengths = (blocks_in - 1) * BLOCK + tail_at
    used = jnp.zeros((loader_count, REACH), jnp.int32)
    offsets = []
    sub_slots = []
    for block_index in range(BLK_DEV):
        starting = breaks[:, block_index] == 1
        wanted = prefs[:, block_index]
        needed = blocks_in[:, block_index]
        used_wanted = jnp.sum(jnp.where(reach_index == wanted[:, None], used, 0), axis=1)
        fits = (wanted == 0) | (needed <= CAP) & (used_wanted + needed <= CAP)
        chosen = jnp.where(fits, wanted, 0)
        used_chosen = jnp.sum(jnp.where(reach_index == chosen[:, None], used, 0), axis=1)
        if block_index == 0:
            offset_now = chosen
            slot_now = used_chosen
        else:
            offset_now = jnp.where(starting, chosen, offsets[-1])
            slot_now = jnp.where(starting, used_chosen, sub_slots[-1] + 1)
        used = used + jnp.where(starting[:, None] & (reach_index == chosen[:, None]), needed[:, None], 0)
        offsets.append(offset_now.astype(jnp.int32))
        sub_slots.append(slot_now.astype(jnp.int32))
    offset_all = jnp.stack(offsets, axis=1)
    sub_all = jnp.stack(sub_slots, axis=1)
    slot_all = jnp.where(offset_all == 0, sub_all, BLK_DEV + (offset_all - 1) * CAP + sub_all)
    owner = (loader_ids // N_REP + offset_all) % N_DP * N_REP + loader_ids % N_REP
    owner_slot = owner * (BLK_DEV + (REACH - 1) * CAP) + slot_all
    return (lengths.reshape(-1).astype(jnp.int32), first.reshape(-1).astype(jnp.int32), owner_slot.reshape(-1).astype(jnp.int32))


def draw_history_length(key, part):
    return routing(key)[0]


def draw_first_block(key, part):
    return routing(key)[1]


def draw_owner_slot(key, part):
    return routing(key)[2]


def shard_levels(key, extent, shards, least, largest):
    loudness = 1.0
    for position, shards_of in shards:
        steps = jax.random.uniform(jax.random.fold_in(jax.random.fold_in(key, 6), position), (shards_of,), jnp.float32, least / len(shards), largest / len(shards))
        loudness = loudness * jnp.repeat(jnp.exp(steps), extent[position] // shards_of).reshape((-1,) + (1,) * (len(extent) - 1 - position))
    return loudness


def centred(key, extent, spread, most, cuts=(), held_as=jnp.bfloat16):
    array = jax.random.normal(key, extent, jnp.float32) * spread
    if len(cuts) > 0:
        array = shard_levels(key, extent, cuts, -0.22, 0.18) * array
    return jnp.clip(array, min=-most, max=most).astype(held_as)


def setup_inputs(seed: int = 0) -> dict:
    key_list = jax.random.split(jax.random.key(seed), 9)
    return {
        "tokens": centred(key_list[0], (TOKENS, D), 1.0, 6.0, ((0, 512),)),
        "owner_cotangent": centred(key_list[1], (OWN_ROWS, D), 1.0, 6.0, ((0, 512),)),
        "proj_weight": centred(key_list[2], (D, 4 * D), D ** -0.5, 0.25),
        "out_weight": centred(key_list[3], (D, D), D ** -0.5, 0.25),
        "bias_table": jnp.clip(jax.random.uniform(key_list[4], (HEADS, BUCKETS), jnp.float32, -1.0, 1.0), -1.0, 1.0),
        "history_length": draw_history_length(jax.random.fold_in(key_list[8], 71), 0),
        "first_block": draw_first_block(jax.random.fold_in(key_list[8], 71), 0),
        "owner_slot": draw_owner_slot(jax.random.fold_in(key_list[8], 71), 0),
    }


EPSILON = 1e-06

def norm_rows(values_in):
    centered = values_in - lax.optimization_barrier(jnp.mean(values_in, axis=-1, keepdims=True))
    inverse = lax.rsqrt(lax.optimization_barrier(jnp.mean(centered * centered, axis=-1, keepdims=True)) + EPSILON)
    return (centered * inverse, inverse)

def norm_back(normed, inverse, upstream):
    return inverse * (upstream - lax.optimization_barrier(jnp.mean(upstream, axis=-1, keepdims=True)) - normed * lax.optimization_barrier(jnp.mean(upstream * normed, axis=-1, keepdims=True)))

def buckets_of(distance):
    bucket = jnp.zeros(distance.shape, jnp.int32)
    for level_index in range(BUCKETS - 1):
        bucket = bucket + (distance >= 2 ** level_index).astype(jnp.int32)
    return bucket

def pair_logits(query_rows, key_rows, bias_table, query_pos, key_pos, seq_length):
    row_count = query_rows.shape[0]
    query_heads = query_rows.reshape(row_count, HEADS, HEAD_DIM).astype(jnp.float32)
    key_heads = key_rows.reshape(row_count, HEADS, HEAD_DIM).astype(jnp.float32)
    scores = jnp.einsum('qhd,khd->hqk', query_heads, key_heads) * HEAD_DIM ** (-0.5)
    distance = query_pos[:, None] - key_pos[None, :]
    onehot = (buckets_of(distance)[:, :, None] == jnp.arange(BUCKETS, dtype=jnp.int32)).astype(jnp.float32)
    bias = jnp.einsum('qkb,hb->hqk', onehot, bias_table, precision=lax.Precision.HIGHEST)
    keep_mask = ((distance >= 0) & (key_pos[None, :] < seq_length) & (query_pos[:, None] < seq_length)).astype(jnp.float32)
    return (scores + bias, keep_mask, onehot, query_heads, key_heads)

def pair_forward(query_rows, key_rows, value_rows, bias_table, query_pos, key_pos, seq_length):
    row_count = query_rows.shape[0]
    logits, keep_mask, onehot, query_heads, key_heads = pair_logits(query_rows, key_rows, bias_table, query_pos, key_pos, seq_length)
    weights = (jax.nn.silu(logits) * keep_mask).astype(jnp.bfloat16)
    value_heads = value_rows.reshape(row_count, HEADS, HEAD_DIM).astype(jnp.float32)
    mixed_heads = jnp.einsum('hqk,khd->qhd', weights.astype(jnp.float32), value_heads)
    return mixed_heads.reshape(row_count, HEADS * HEAD_DIM)

def pair_backward(query_rows, key_rows, value_rows, upstream, bias_table, query_pos, key_pos, seq_length):
    row_count = query_rows.shape[0]
    logits, keep_mask, onehot, query_heads, key_heads = pair_logits(query_rows, key_rows, bias_table, query_pos, key_pos, seq_length)
    sigma = jax.nn.sigmoid(logits)
    weights = (jax.nn.silu(logits) * keep_mask).astype(jnp.bfloat16)
    value_heads = value_rows.reshape(row_count, HEADS, HEAD_DIM).astype(jnp.float32)
    upstream_heads = upstream.reshape(row_count, HEADS, HEAD_DIM).astype(jnp.float32)
    d_weights = jnp.einsum('qhd,khd->hqk', upstream_heads, value_heads)
    d_logits = d_weights * keep_mask * sigma * (1.0 + logits * (1.0 - sigma))
    d_table = jnp.einsum('hqk,qkb->hb', d_logits, onehot, precision=lax.Precision.HIGHEST)
    d_logits_b = d_logits.astype(jnp.bfloat16).astype(jnp.float32)
    d_query = jnp.einsum('hqk,khd->qhd', d_logits_b, key_heads) * HEAD_DIM ** (-0.5)
    d_key = jnp.einsum('hqk,qhd->khd', d_logits_b, query_heads) * HEAD_DIM ** (-0.5)
    d_value = jnp.einsum('hqk,qhd->khd', weights.astype(jnp.float32), upstream_heads)
    width_all = HEADS * HEAD_DIM
    return (d_query.reshape(row_count, width_all), d_key.reshape(row_count, width_all), d_value.reshape(row_count, width_all), d_table)

def pick(stacked, where_at):
    return lax.dynamic_index_in_dim(stacked, where_at, 0, keepdims=False)

def add_at(stacked, where_at, addend):
    return lax.dynamic_update_index_in_dim(stacked, pick(stacked, where_at) + addend, where_at, 0)

def layer_grads(block_rows, cot_blocks, lengths, positions, proj_weight, out_weight, bias_table):
    block_count, row_count, model_width = block_rows.shape
    flat_rows = block_count * row_count
    inputs = block_rows.reshape(flat_rows, model_width).astype(jnp.float32)
    token_pos = positions[:, None] * row_count + jnp.arange(row_count, dtype=jnp.int32)[None, :]
    valid = (token_pos < lengths[:, None]).reshape(flat_rows, 1)
    normed, inverse = norm_rows(inputs)
    normed_b = normed.astype(jnp.bfloat16)
    proj = jnp.dot(normed_b, proj_weight, preferred_element_type=jnp.float32)
    sigma = jax.nn.sigmoid(proj)
    acts = jax.nn.silu(proj).astype(jnp.bfloat16)
    gate_part = acts[:, :model_width]
    value_part = acts[:, model_width:2 * model_width].reshape(block_count, row_count, model_width)
    query_part = acts[:, 2 * model_width:3 * model_width].reshape(block_count, row_count, model_width)
    key_part = acts[:, 3 * model_width:].reshape(block_count, row_count, model_width)
    first_of = jnp.arange(block_count, dtype=jnp.int32) - positions
    lower_rows, lower_cols = np.tril_indices(block_count)
    lower_rows = jnp.asarray(lower_rows, jnp.int32)
    lower_cols = jnp.asarray(lower_cols, jnp.int32)
    is_live = (first_of[lower_rows] == first_of[lower_cols]) & (lengths[lower_rows] > 0)
    order = jnp.argsort(jnp.where(is_live, 0, 1), stable=True)
    pair_query = lower_rows[order].astype(jnp.int32)
    pair_key = lower_cols[order].astype(jnp.int32)
    live_pairs = jnp.sum(is_live.astype(jnp.int32))

    def forward_step(step_index, attended):
        query_block = pair_query[step_index]
        key_block = pair_key[step_index]
        addend = pair_forward(pick(query_part, query_block), pick(key_part, key_block), pick(value_part, key_block), bias_table, pick(token_pos, query_block), pick(token_pos, key_block), pick(lengths, query_block))
        return add_at(attended, query_block, addend)
    attended = lax.fori_loop(0, live_pairs, forward_step, jnp.zeros((block_count, row_count, model_width), jnp.float32))
    att_n, att_inverse = norm_rows(attended.reshape(flat_rows, model_width))
    gate_float = gate_part.astype(jnp.float32)
    mixed = (att_n * gate_float).astype(jnp.bfloat16)
    upstream = jnp.where(valid, cot_blocks.reshape(flat_rows, model_width), 0)
    out_grad = jnp.dot(mixed.T, upstream, preferred_element_type=jnp.float32)
    d_mixed = jnp.dot(upstream, out_weight.T, preferred_element_type=jnp.float32)
    d_gate = d_mixed * att_n
    d_attended = norm_back(att_n, att_inverse, d_mixed * gate_float).astype(jnp.bfloat16)
    d_attended = d_attended.reshape(block_count, row_count, model_width)

    def backward_step(step_index, carry):
        d_query, d_key, d_value, d_table = carry
        query_block = pair_query[step_index]
        key_block = pair_key[step_index]
        grads = pair_backward(pick(query_part, query_block), pick(key_part, key_block), pick(value_part, key_block), pick(d_attended, query_block), bias_table, pick(token_pos, query_block), pick(token_pos, key_block), pick(lengths, query_block))
        return (add_at(d_query, query_block, grads[0]), add_at(d_key, key_block, grads[1]), add_at(d_value, key_block, grads[2]), d_table + grads[3])
    zero_blocks = jnp.zeros((block_count, row_count, model_width), jnp.float32)
    d_query, d_key, d_value, bias_grad = lax.fori_loop(0, live_pairs, backward_step, (zero_blocks, zero_blocks, zero_blocks, jnp.zeros((HEADS, BUCKETS), jnp.float32)))
    d_acts = jnp.concatenate([d_gate, d_value.reshape(flat_rows, model_width), d_query.reshape(flat_rows, model_width), d_key.reshape(flat_rows, model_width)], axis=1)
    d_proj = (d_acts * sigma * (1.0 + proj * (1.0 - sigma))).astype(jnp.bfloat16)
    proj_grad = jnp.dot(normed_b.T, d_proj, preferred_element_type=jnp.float32)
    d_normed = jnp.dot(d_proj, proj_weight.T, preferred_element_type=jnp.float32)
    token_grad = (upstream.astype(jnp.float32) + norm_back(normed, inverse, d_normed)).astype(jnp.bfloat16)
    return (token_grad, proj_grad, out_grad, bias_grad)

def reference(tokens, owner_cotangent, proj_weight, out_weight, bias_table, history_length, first_block, owner_slot):
    loader_count = N_DP * N_REP
    model_width = tokens.shape[1]
    loader_rows = tokens.reshape(loader_count, BLK_DEV, BLOCK, model_width)
    owner_blocks = owner_cotangent.reshape(-1, BLOCK, model_width)
    cot_rows = owner_blocks[owner_slot.astype(jnp.int32)].reshape(loader_count, BLK_DEV, BLOCK, model_width)
    lengths = history_length.reshape(loader_count, BLK_DEV)
    positions = jnp.arange(BLK_DEV, dtype=jnp.int32)[None, :] - first_block.reshape(loader_count, BLK_DEV)

    def one_loader(carry, item):
        token_grad, proj_grad, out_grad, bias_grad = layer_grads(item[0], item[1], item[2], item[3], proj_weight, out_weight, bias_table)
        return ((carry[0] + proj_grad, carry[1] + out_grad, carry[2] + bias_grad), token_grad)
    start_sums = (jnp.zeros((model_width, 4 * model_width), jnp.float32), jnp.zeros((model_width, model_width), jnp.float32), jnp.zeros((HEADS, BUCKETS), jnp.float32))
    sums, token_grad = lax.scan(one_loader, start_sums, (loader_rows, cot_rows, lengths, positions))
    return (token_grad.reshape(TOKENS, model_width), sums[0], sums[1], sums[2])
```

```python
import jax
import jax.numpy as jnp
from jax import lax
from jax.experimental import pallas as pl
from jax.experimental.pallas import tpu as pltpu
from jax.sharding import PartitionSpec as P

HEADS = 4
HEAD_DIM = 128
BLOCK = 128
BLOCKS = 4
SLOTS = 6
BUCKETS = 10
D = 512
ROWS = BLOCKS * BLOCK
EPSILON = 1e-06
SCALE = HEAD_DIM ** (-0.5)
BF16 = jnp.bfloat16
F32 = jnp.float32
BUCKETS_AT = (range(0, 8), range(1, 9), range(8, 10), range(9, 10))


def dot(a, b):
    return lax.dot_general(a, b, (((1,), (0,)), ((), ())), preferred_element_type=F32)


def dot_right_t(a, b):
    return lax.dot_general(a, b, (((1,), (1,)), ((), ())), preferred_element_type=F32)


def dot_left_t(a, b):
    return lax.dot_general(a, b, (((0,), (0,)), ((), ())), preferred_element_type=F32)


def row_sum(parts):
    total = parts[0]
    for part in parts[1:]:
        total = total + part
    return jnp.sum(total, axis=-1, keepdims=True)


def tile_iota(axis):
    return lax.broadcasted_iota(jnp.int32, (BLOCK, BLOCK), axis)


def norm_tokens(tokens_ref, normed_ref, normed_b_ref, inverse_ref):
    def body(b, carry):
        rows = pl.ds(pl.multiple_of(b * BLOCK, BLOCK), BLOCK)
        x = tokens_ref[rows, :].astype(F32)
        centered = x - jnp.mean(x, axis=-1, keepdims=True)
        inverse = lax.rsqrt(jnp.mean(centered * centered, axis=-1, keepdims=True) + EPSILON)
        normed = centered * inverse
        normed_ref[rows, :] = normed
        normed_b_ref[rows, :] = normed.astype(BF16)
        inverse_ref[rows, :] = jnp.broadcast_to(inverse, (BLOCK, BLOCK))
        return carry

    lax.fori_loop(0, BLOCKS, body, 0)


def project(normed_b_ref, weight_ref, acts_ref, slope_ref):
    def body(c, carry):
        columns = pl.ds(pl.multiple_of(c * 256, 256), 256)
        half = dot(normed_b_ref[...], weight_ref[:, columns]) * 0.5
        u = 1.0 + jnp.tanh(half)
        act = half * u
        slope = 0.5 * (u + act * (2.0 - u))
        act = act.astype(BF16)
        for k in range(2):
            acts_ref[2 * c + k] = act[:, k * 128 : (k + 1) * 128]
            slope_ref[2 * c + k] = slope[:, k * 128 : (k + 1) * 128]
        return carry

    lax.fori_loop(0, 8, body, 0)


def take_upstream(own_ref, received_ref, slot_ref, length_ref, first_ref, upstream_ref):
    def body(b, carry):
        rows = pl.ds(pl.multiple_of(b * BLOCK, BLOCK), BLOCK)
        slot = lax.rem(slot_ref[b], SLOTS)
        own_at = pl.multiple_of(jnp.minimum(slot, 3) * BLOCK, BLOCK)
        received_at = pl.multiple_of(jnp.maximum(slot - 4, 0) * BLOCK, BLOCK)
        own = own_ref[pl.ds(own_at, BLOCK), :].astype(F32)
        received = received_ref[pl.ds(received_at, BLOCK), :].astype(F32)
        limit = length_ref[b] - (b - first_ref[b]) * BLOCK
        row = lax.broadcasted_iota(jnp.int32, (BLOCK, D), 0)
        is_own = jnp.full((BLOCK, D), slot, jnp.int32) < 4
        value = jnp.where(row < limit, jnp.where(is_own, own, received), 0.0)
        upstream_ref[rows, :] = value.astype(BF16)
        return carry

    lax.fori_loop(0, BLOCKS, body, 0)


def mix_back(upstream_ref, out_weight_ref, d_mixed_ref):
    for c in range(2):
        part = dot_right_t(upstream_ref[...], out_weight_ref[c * 256 : (c + 1) * 256, :])
        for k in range(2):
            d_mixed_ref[2 * c + k] = part[:, k * 128 : (k + 1) * 128]


def bucket_bounds(apart):
    distance = tile_iota(0) - tile_iota(1) + apart * BLOCK
    return distance, [(bucket, 0 if bucket == 0 else 2 ** (bucket - 1)) for bucket in BUCKETS_AT[apart]]


def bias_tiles(table_ref, head):
    tiles = []
    for apart in range(BLOCKS):
        distance, bounds = bucket_bounds(apart)
        tile = jnp.full((BLOCK, BLOCK), table_ref[head, bounds[0][0]] * 0.5, F32)
        for bucket, least in bounds[1:]:
            tile = jnp.where(distance >= least, table_ref[head, bucket] * 0.5, tile)
        tiles.append(tile)
    return tiles


def attend(acts_ref, table_ref, length_ref, first_ref, weights_ref, factor_ref, attended_ref):
    def body(head, carry):
        bias = bias_tiles(table_ref, head)
        row = tile_iota(0)
        causal_row = jnp.where(tile_iota(1) <= row, row, ROWS)
        for i in range(BLOCKS):
            rows = pl.ds(i * BLOCK, BLOCK)
            upto = (i + 1) * BLOCK
            scores = dot_right_t(acts_ref[8 + head, rows, :], acts_ref[12 + head, 0:upto, :])
            for j in range(i + 1):
                lanes = pl.ds(j * BLOCK, BLOCK)
                limit = jnp.where(
                    first_ref[i] == first_ref[j], length_ref[i] - (i - first_ref[i]) * BLOCK, 0
                )
                half = scores[:, j * BLOCK : (j + 1) * BLOCK] * (0.5 * SCALE) + bias[i - j]
                kept = (causal_row if i == j else row) < limit
                u = jnp.where(kept, 1.0 + jnp.tanh(half), 0.0)
                weight = half * u
                factor_ref[head, rows, lanes] = 0.5 * (u + weight * (2.0 - u))
                weights_ref[head, rows, lanes] = weight.astype(BF16)
            attended_ref[head, rows, :] = dot(
                weights_ref[head, rows, 0:upto], acts_ref[4 + head, 0:upto, :]
            )
        return carry

    lax.fori_loop(0, HEADS, body, 0)


def mix(acts_ref, attended_ref, d_mixed_ref, slope_ref, mixed_ref, d_attended_ref, d_proj_ref):
    def body(b, carry):
        rows = pl.ds(pl.multiple_of(b * BLOCK, BLOCK), BLOCK)
        heads = range(HEADS)
        att = [attended_ref[h, rows, :] for h in heads]
        mean = row_sum(att) * (1.0 / D)
        centered = [a - mean for a in att]
        inverse = lax.rsqrt(row_sum([c * c for c in centered]) * (1.0 / D) + EPSILON)
        normed = [c * inverse for c in centered]
        gate = [acts_ref[h, rows, :].astype(F32) for h in heads]
        d_mixed = [d_mixed_ref[h, rows, :] for h in heads]
        g = [d_mixed[h] * gate[h] for h in heads]
        g_mean = row_sum(g) * (1.0 / D)
        g_dot = row_sum([g[h] * normed[h] for h in heads]) * (1.0 / D)
        for h in heads:
            lanes = pl.ds(h * 128, 128)
            mixed_ref[rows, lanes] = (normed[h] * gate[h]).astype(BF16)
            d_attended_ref[h, rows, :] = (inverse * (g[h] - g_mean - normed[h] * g_dot)).astype(BF16)
            d_proj_ref[rows, lanes] = (d_mixed[h] * normed[h] * slope_ref[h, rows, :]).astype(BF16)
        return carry

    lax.fori_loop(0, BLOCKS, body, 0)


def attend_back(
    acts_ref, weights_ref, factor_ref, d_attended_ref, slope_ref, d_logits_ref, d_proj_ref, bias_ref
):
    def body(head, carry):
        sums = [None] * BLOCKS
        for i in range(BLOCKS):
            rows = pl.ds(i * BLOCK, BLOCK)
            upto = (i + 1) * BLOCK
            d_weights = dot_right_t(d_attended_ref[head, rows, :], acts_ref[4 + head, 0:upto, :])
            for j in range(i + 1):
                lanes = pl.ds(j * BLOCK, BLOCK)
                d_logits = d_weights[:, j * BLOCK : (j + 1) * BLOCK] * factor_ref[head, rows, lanes]
                sums[i - j] = d_logits if sums[i - j] is None else sums[i - j] + d_logits
                d_logits_ref[rows, lanes] = d_logits.astype(BF16)
            d_query = dot(d_logits_ref[rows, 0:upto], acts_ref[12 + head, 0:upto, :])
            at = pl.ds(pl.multiple_of(1024 + head * 128, 128), 128)
            d_proj_ref[rows, at] = (d_query * SCALE * slope_ref[8 + head, rows, :]).astype(BF16)
        for j in range(BLOCKS):
            rows = pl.ds(j * BLOCK, BLOCK)
            below = pl.ds(j * BLOCK, ROWS - j * BLOCK)
            d_value = dot_left_t(weights_ref[head, below, rows], d_attended_ref[head, below, :])
            at = pl.ds(pl.multiple_of(512 + head * 128, 128), 128)
            d_proj_ref[rows, at] = (d_value * slope_ref[4 + head, rows, :]).astype(BF16)
            d_key = dot_left_t(d_logits_ref[below, rows], acts_ref[8 + head, below, :])
            at = pl.ds(pl.multiple_of(1536 + head * 128, 128), 128)
            d_proj_ref[rows, at] = (d_key * SCALE * slope_ref[12 + head, rows, :]).astype(BF16)
        totals = [None] * BUCKETS
        for apart in range(BLOCKS):
            distance, bounds = bucket_bounds(apart)
            for at, (bucket, least) in enumerate(bounds):
                value = sums[apart]
                if at > 0:
                    value = jnp.where(distance >= least, value, 0.0)
                if at + 1 < len(bounds):
                    value = jnp.where(distance < bounds[at + 1][1], value, 0.0)
                value = jnp.sum(value, axis=0, keepdims=True)
                totals[bucket] = value if totals[bucket] is None else totals[bucket] + value
        lane = lax.broadcasted_iota(jnp.int32, (1, 128), 1)
        packed = jnp.zeros((1, 128), F32)
        for bucket in range(BUCKETS):
            packed = jnp.where(lane == bucket, jnp.sum(totals[bucket], axis=1, keepdims=True), packed)
        bias_ref[pl.ds(head, 1), :] = packed
        return carry

    lax.fori_loop(0, HEADS, body, 0)


def weight_grads(normed_b_ref, d_proj_ref, proj_term_ref):
    def body(c, carry):
        at = pl.ds(pl.multiple_of(c * 256, 256), 256)
        proj_term_ref[at, :] = dot_left_t(d_proj_ref[:, at], normed_b_ref[...]).astype(
            proj_term_ref.dtype
        )
        return carry

    lax.fori_loop(0, 8, body, 0)


def token_grads(d_proj_ref, weight_ref, normed_ref, inverse_ref, upstream_ref, token_grad_ref):
    def body(b, carry):
        rows = pl.ds(pl.multiple_of(b * 256, 256), 256)
        d_normed = dot_right_t(d_proj_ref[rows, :], weight_ref[...])
        normed = normed_ref[rows, :]
        inverse = inverse_ref[rows, 0:1]
        mean = jnp.mean(d_normed, axis=-1, keepdims=True)
        along = jnp.mean(d_normed * normed, axis=-1, keepdims=True)
        back = inverse * (d_normed - mean - normed * along)
        token_grad_ref[rows, :] = (upstream_ref[rows, :].astype(F32) + back).astype(BF16)
        return carry

    lax.fori_loop(0, 2, body, 0)


def layer_kernel(
    tokens_ref,
    own_ref,
    received_ref,
    weight_ref,
    out_weight_ref,
    table_ref,
    length_ref,
    first_ref,
    slot_ref,
    token_grad_ref,
    proj_term_ref,
    out_term_ref,
    bias_ref,
    normed_ref,
    normed_b_ref,
    inverse_ref,
    acts_ref,
    slope_ref,
    upstream_ref,
    d_mixed_ref,
    weights_ref,
    factor_ref,
    attended_ref,
    mixed_ref,
    d_attended_ref,
    d_logits_ref,
    d_proj_ref,
):
    norm_tokens(tokens_ref, normed_ref, normed_b_ref, inverse_ref)
    project(normed_b_ref, weight_ref, acts_ref, slope_ref)
    attend(acts_ref, table_ref, length_ref, first_ref, weights_ref, factor_ref, attended_ref)
    take_upstream(own_ref, received_ref, slot_ref, length_ref, first_ref, upstream_ref)
    mix_back(upstream_ref, out_weight_ref, d_mixed_ref)
    mix(acts_ref, attended_ref, d_mixed_ref, slope_ref, mixed_ref, d_attended_ref, d_proj_ref)
    out_term_ref[...] = dot_left_t(mixed_ref[...], upstream_ref[...]).astype(out_term_ref.dtype)
    bias_ref[...] = jnp.zeros_like(bias_ref)
    attend_back(
        acts_ref, weights_ref, factor_ref, d_attended_ref, slope_ref, d_logits_ref, d_proj_ref, bias_ref
    )
    weight_grads(normed_b_ref, d_proj_ref, proj_term_ref)
    token_grads(d_proj_ref, weight_ref, normed_ref, inverse_ref, upstream_ref, token_grad_ref)


LAYER_SCRATCH = [
    pltpu.VMEM((ROWS, D), F32),
    pltpu.VMEM((ROWS, D), BF16),
    pltpu.VMEM((ROWS, BLOCK), F32),
    pltpu.VMEM((16, ROWS, 128), BF16),
    pltpu.VMEM((16, ROWS, 128), F32),
    pltpu.VMEM((ROWS, D), BF16),
    pltpu.VMEM((HEADS, ROWS, 128), F32),
    pltpu.VMEM((HEADS, ROWS, ROWS), BF16),
    pltpu.VMEM((HEADS, ROWS, ROWS), F32),
    pltpu.VMEM((HEADS, ROWS, 128), F32),
    pltpu.VMEM((ROWS, D), BF16),
    pltpu.VMEM((HEADS, ROWS, 128), BF16),
    pltpu.VMEM((ROWS, ROWS), BF16),
    pltpu.VMEM((ROWS, 4 * D), BF16),
]


def layer_grads(tokens, own, received, weight, out_weight, table, length, first, slot, term_type):
    vmem = pl.BlockSpec(memory_space=pltpu.VMEM)
    smem = pl.BlockSpec(memory_space=pltpu.SMEM)
    return pl.pallas_call(
        layer_kernel,
        out_shape=(
            jax.ShapeDtypeStruct((ROWS, D), BF16),
            jax.ShapeDtypeStruct((4 * D, D), term_type),
            jax.ShapeDtypeStruct((D, D), term_type),
            jax.ShapeDtypeStruct((8, 128), F32),
        ),
        in_specs=[vmem] * 5 + [smem] * 4,
        out_specs=(vmem,) * 4,
        scratch_shapes=LAYER_SCRATCH,
        compiler_params=pltpu.CompilerParams(vmem_limit_bytes=52 * 2**20),
        name="layer_grads",
    )(tokens, own, received, weight, out_weight, table, length, first, slot)


def shards(tokens, cotangent, weight, out_weight, table, length, first, slot):
    count = lax.axis_size("dp")
    received = lax.ppermute(
        cotangent[ROWS:], "dp", [(source, (source - 1) % count) for source in range(count)]
    )
    token_grad, proj_term, out_term, bias_term = layer_grads(
        tokens, cotangent, received, weight, out_weight, table, length, first, slot, F32
    )
    proj_grad = lax.psum_scatter(proj_term, ("dp", "rep"), scatter_dimension=0, tiled=True)
    out_grad, bias_grad = lax.psum((out_term, bias_term), ("dp", "rep"))
    return token_grad, proj_grad.T, out_grad, bias_grad[:HEADS, :BUCKETS]


def solution(mesh):
    split = P(("dp", "rep"))
    return jax.shard_map(
        shards,
        mesh=mesh,
        in_specs=(split, split, P(), P(), P(), split, split, split),
        out_specs=(split, P(None, ("dp", "rep")), P(), P()),
        check_vma=False,
    )
```

```python
import jax
import jax.numpy as jnp
from jax import lax
from jax.experimental import pallas as pl
from jax.experimental.pallas import tpu as pltpu
from jax.sharding import PartitionSpec as P

HEADS = 4
HEAD_DIM = 128
BLOCK = 128
BLOCKS = 4
SLOTS = 6
BUCKETS = 10
NX, NY, NZ = 4, 8, 8
SETS = HEADS + 1
D = 512
ROWS = BLOCKS * BLOCK
EPSILON = 1e-06
SCALE = HEAD_DIM ** (-0.5)
BF16 = jnp.bfloat16
F32 = jnp.float32
GATE, VALUE, QUERY, KEY = (slice(g * 128, (g + 1) * 128) for g in range(4))
BUCKETS_AT = (range(0, 8), range(1, 9), range(8, 10), range(9, 10))


def dot(a, b):
    return lax.dot_general(a, b, (((1,), (0,)), ((), ())), preferred_element_type=F32)


def dot_right_t(a, b):
    return lax.dot_general(a, b, (((1,), (1,)), ((), ())), preferred_element_type=F32)


def dot_left_t(a, b):
    return lax.dot_general(a, b, (((0,), (0,)), ((), ())), preferred_element_type=F32)


def row_sum(parts):
    total = parts[0]
    for part in parts[1:]:
        total = total + part
    return jnp.sum(total, axis=-1, keepdims=True)


def tile_iota(axis):
    return lax.broadcasted_iota(jnp.int32, (BLOCK, BLOCK), axis)


def norm_tokens(tokens_ref, normed_ref, normed_b_ref, inverse_ref):
    def body(b, carry):
        rows = pl.ds(pl.multiple_of(b * BLOCK, BLOCK), BLOCK)
        x = tokens_ref[rows, :].astype(F32)
        centered = x - jnp.mean(x, axis=-1, keepdims=True)
        inverse = lax.rsqrt(jnp.mean(centered * centered, axis=-1, keepdims=True) + EPSILON)
        normed = centered * inverse
        normed_ref[rows, :] = normed
        normed_b_ref[rows, :] = normed.astype(BF16)
        inverse_ref[rows, :] = jnp.broadcast_to(inverse, (BLOCK, BLOCK))
        return carry

    lax.fori_loop(0, BLOCKS, body, 0)


def project(head, normed_b_ref, weight_ref, acts_ref, slope_ref):
    for c in range(2):
        lanes = pl.ds(c * 256, 256)
        half = dot(normed_b_ref[...], weight_ref[head, :, lanes]) * 0.5
        u = 1.0 + jnp.tanh(half)
        act = half * u
        slope_ref[head, :, lanes] = 0.5 * (u + act * (2.0 - u))
        acts_ref[head, :, lanes] = act.astype(BF16)


def take_upstream(own_ref, received_ref, slot_ref, length_ref, first_ref, upstream_ref):
    def body(b, carry):
        rows = pl.ds(pl.multiple_of(b * BLOCK, BLOCK), BLOCK)
        slot = jnp.full((BLOCK, D), lax.rem(slot_ref[b], SLOTS), jnp.int32)
        value = own_ref[0:BLOCK, :].astype(F32)
        for at in range(1, SLOTS):
            ref, row_at = (own_ref, at * BLOCK) if at < BLOCKS else (received_ref, (at - BLOCKS) * BLOCK)
            value = jnp.where(slot == at, ref[row_at : row_at + BLOCK, :].astype(F32), value)
        limit = length_ref[b] - (b - first_ref[b]) * BLOCK
        row = lax.broadcasted_iota(jnp.int32, (BLOCK, D), 0)
        value = jnp.where(row < limit, value, 0.0)
        upstream_ref[rows, :] = value.astype(BF16)
        return carry

    lax.fori_loop(0, BLOCKS, body, 0)


def mix_back(upstream_ref, out_weight_ref, d_mixed_ref):
    for c in range(2):
        part = dot_right_t(upstream_ref[...], out_weight_ref[c * 256 : (c + 1) * 256, :])
        for k in range(2):
            d_mixed_ref[2 * c + k] = part[:, k * 128 : (k + 1) * 128]


def bucket_bounds(apart):
    distance = tile_iota(0) - tile_iota(1) + apart * BLOCK
    return distance, [(bucket, 0 if bucket == 0 else 2 ** (bucket - 1)) for bucket in BUCKETS_AT[apart]]


def bias_tiles(table_ref, head):
    tiles = []
    for apart in range(BLOCKS):
        distance, bounds = bucket_bounds(apart)
        tile = jnp.full((BLOCK, BLOCK), table_ref[head, bounds[0][0]] * 0.5, F32)
        for bucket, least in bounds[1:]:
            tile = jnp.where(distance >= least, table_ref[head, bucket] * 0.5, tile)
        tiles.append(tile)
    return tiles


def attend(head, acts_ref, table_ref, length_ref, first_ref, weights_ref, factor_ref, attended_ref):
    bias = bias_tiles(table_ref, head)
    row = tile_iota(0)
    causal_row = jnp.where(tile_iota(1) <= row, row, ROWS)
    for i in range(BLOCKS):
        rows = pl.ds(i * BLOCK, BLOCK)
        upto = (i + 1) * BLOCK
        scores = dot_right_t(acts_ref[head, rows, QUERY], acts_ref[head, 0:upto, KEY])
        for j in range(i + 1):
            lanes = pl.ds(j * BLOCK, BLOCK)
            limit = jnp.where(
                first_ref[i] == first_ref[j], length_ref[i] - (i - first_ref[i]) * BLOCK, 0
            )
            half = scores[:, j * BLOCK : (j + 1) * BLOCK] * (0.5 * SCALE) + bias[i - j]
            kept = (causal_row if i == j else row) < limit
            u = jnp.where(kept, 1.0 + jnp.tanh(half), 0.0)
            weight = half * u
            factor_ref[head, rows, lanes] = 0.5 * (u + weight * (2.0 - u))
            weights_ref[head, rows, lanes] = weight.astype(BF16)
        attended_ref[head, rows, :] = dot(
            weights_ref[head, rows, 0:upto], acts_ref[head, 0:upto, VALUE]
        )


def mix(acts_ref, attended_ref, d_mixed_ref, slope_ref, mixed_ref, d_attended_ref, d_proj_ref):
    def body(b, carry):
        rows = pl.ds(pl.multiple_of(b * BLOCK, BLOCK), BLOCK)
        heads = range(HEADS)
        att = [attended_ref[h, rows, :] for h in heads]
        mean = row_sum(att) * (1.0 / D)
        centered = [a - mean for a in att]
        inverse = lax.rsqrt(row_sum([c * c for c in centered]) * (1.0 / D) + EPSILON)
        normed = [c * inverse for c in centered]
        gate = [acts_ref[h, rows, GATE].astype(F32) for h in heads]
        d_mixed = [d_mixed_ref[h, rows, :] for h in heads]
        g = [d_mixed[h] * gate[h] for h in heads]
        g_mean = row_sum(g) * (1.0 / D)
        g_dot = row_sum([g[h] * normed[h] for h in heads]) * (1.0 / D)
        for h in heads:
            mixed_ref[rows, pl.ds(h * 128, 128)] = (normed[h] * gate[h]).astype(BF16)
            d_attended_ref[h, rows, :] = (inverse * (g[h] - g_mean - normed[h] * g_dot)).astype(BF16)
            d_proj_ref[h, rows, GATE] = (d_mixed[h] * normed[h] * slope_ref[h, rows, GATE]).astype(BF16)
        return carry

    lax.fori_loop(0, BLOCKS, body, 0)


def attend_back(
    head, acts_ref, weights_ref, factor_ref, d_attended_ref, slope_ref, d_logits_ref, d_proj_ref, bias_ref
):
    sums = [None] * BLOCKS
    for i in range(BLOCKS):
        rows = pl.ds(i * BLOCK, BLOCK)
        upto = (i + 1) * BLOCK
        d_weights = dot_right_t(d_attended_ref[head, rows, :], acts_ref[head, 0:upto, VALUE])
        for j in range(i + 1):
            lanes = pl.ds(j * BLOCK, BLOCK)
            d_logits = d_weights[:, j * BLOCK : (j + 1) * BLOCK] * factor_ref[head, rows, lanes]
            sums[i - j] = d_logits if sums[i - j] is None else sums[i - j] + d_logits
            d_logits_ref[rows, lanes] = d_logits.astype(BF16)
        d_query = dot(d_logits_ref[rows, 0:upto], acts_ref[head, 0:upto, KEY])
        d_proj_ref[head, rows, QUERY] = (d_query * SCALE * slope_ref[head, rows, QUERY]).astype(BF16)
    for j in range(BLOCKS):
        rows = pl.ds(j * BLOCK, BLOCK)
        below = pl.ds(j * BLOCK, ROWS - j * BLOCK)
        d_value = dot_left_t(weights_ref[head, below, rows], d_attended_ref[head, below, :])
        d_proj_ref[head, rows, VALUE] = (d_value * slope_ref[head, rows, VALUE]).astype(BF16)
        d_key = dot_left_t(d_logits_ref[below, rows], acts_ref[head, below, QUERY])
        d_proj_ref[head, rows, KEY] = (d_key * SCALE * slope_ref[head, rows, KEY]).astype(BF16)
    totals = [None] * BUCKETS
    for apart in range(BLOCKS):
        distance, bounds = bucket_bounds(apart)
        for at, (bucket, least) in enumerate(bounds):
            value = sums[apart]
            if at > 0:
                value = jnp.where(distance >= least, value, 0.0)
            if at + 1 < len(bounds):
                value = jnp.where(distance < bounds[at + 1][1], value, 0.0)
            value = jnp.sum(value, axis=0, keepdims=True)
            totals[bucket] = value if totals[bucket] is None else totals[bucket] + value
    lane = lax.broadcasted_iota(jnp.int32, (1, 128), 1)
    packed = jnp.zeros((1, 128), F32)
    for bucket in range(BUCKETS):
        packed = jnp.where(lane == bucket, jnp.sum(totals[bucket], axis=1, keepdims=True), packed)
    bias_ref[pl.ds(head, 1), :] = packed


def token_grads(part, d_proj_ref, weight_ref, normed_ref, inverse_ref, upstream_ref, token_grad_ref):
    rows = pl.ds(part * 256, 256)
    d_normed = dot_right_t(d_proj_ref[0, rows, :], weight_ref[0])
    for h in range(1, HEADS):
        d_normed = d_normed + dot_right_t(d_proj_ref[h, rows, :], weight_ref[h])
    normed = normed_ref[rows, :]
    inverse = inverse_ref[rows, 0:1]
    mean = jnp.mean(d_normed, axis=-1, keepdims=True)
    along = jnp.mean(d_normed * normed, axis=-1, keepdims=True)
    back = inverse * (d_normed - mean - normed * along)
    token_grad_ref[rows, :] = (upstream_ref[rows, :].astype(F32) + back).astype(BF16)


def place():
    dp = lax.axis_index("dp")
    return lax.axis_index("rep"), lax.div(dp, 2 * NZ), lax.rem(lax.div(dp, 2), NZ), lax.rem(dp, 2)


def device(x, y, z, core):
    return ((y * NZ + z) * 2 + core, x)


def layer_kernel(
    tokens_hbm, cotangent_hbm, weight_hbm, out_weight_hbm, table_hbm, length_hbm, first_hbm, slot_hbm,
    token_grad_ref, proj_grad_ref, out_grad_ref, bias_grad_ref,
    tokens_ref, own_ref, received_ref, weight_ref, out_weight_ref, table_ref, length_ref, first_ref, slot_ref,
    normed_ref, normed_b_ref, inverse_ref, acts_ref, slope_ref, upstream_ref, d_mixed_ref, weights_ref,
    factor_ref, attended_ref, mixed_ref, d_attended_ref, d_logits_ref, d_proj_ref,
    term, core_in, x_out, x_in, x_sum, y_in, y_sum, z_in, column_sum, column_in,
    out_y_in, out_z_all, out_mine, out_x_all, out_core_in,
    bias_core, bias_x, bias_y, bias_z,
    load_sem, cotangent_sem, core_sem, x_sem, y_send, y_recv, z_sem, column_sem,
    out_y_sem, out_z_sem, out_y_back_sem, out_x_back_sem, out_core_back_sem,
    bias_core_sem, bias_x_sem, bias_y_sem, bias_z_sem,
):
    x, y, z, core = place()
    other = 1 - core
    dp = lax.axis_index("dp")
    n_dp = 2 * NY * NZ

    def x_peer(k):
        return lax.rem(x + k, NX)

    def y_peer(k):
        return lax.rem(y + k, NY)

    def z_peer(k):
        return lax.rem(z + k, NZ)

    def remote(src, dst, send, recv, target):
        return pltpu.make_async_remote_copy(
            src_ref=src, dst_ref=dst, send_sem=send, recv_sem=recv, device_id=target,
            device_id_type=pl.DeviceIdType.MESH,
        )

    loads = [
        pltpu.make_async_copy(tokens_hbm, tokens_ref, load_sem.at[0]),
        pltpu.make_async_copy(table_hbm, table_ref, load_sem.at[1]),
        pltpu.make_async_copy(length_hbm, length_ref, load_sem.at[2]),
        pltpu.make_async_copy(first_hbm, first_ref, load_sem.at[3]),
        pltpu.make_async_copy(slot_hbm, slot_ref, load_sem.at[4]),
        pltpu.make_async_copy(cotangent_hbm.at[pl.ds(0, ROWS)], own_ref, load_sem.at[5]),
        pltpu.make_async_copy(out_weight_hbm, out_weight_ref, load_sem.at[6]),
    ]
    weight_loads = [
        pltpu.make_async_copy(
            weight_hbm.at[:, pl.ds(g * D + h * 128, 128)],
            weight_ref.at[h, :, pl.ds(g * 128, 128)],
            load_sem.at[7 + h * 4 + g],
        )
        for h in range(HEADS)
        for g in range(4)
    ]
    for load in loads[:1] + weight_loads + loads[1:]:
        load.start()

    barrier = pltpu.get_barrier_semaphore()
    greeted = [device(x, y, z, other)]
    greeted += [device(x_peer(k), y, z, core) for k in range(1, NX)]
    greeted += [device(x, y_peer(k), z, core) for k in range(1, NY)]
    greeted += [device(x, y, z_peer(k), core) for k in range(1, NZ)]
    greeted += [(lax.rem(dp + n_dp + 2 * core - 1, n_dp), x)]
    for target in greeted:
        pl.semaphore_signal(barrier, inc=1, device_id=target, device_id_type=pl.DeviceIdType.MESH)

    loads[0].wait()
    norm_tokens(tokens_ref, normed_ref, normed_b_ref, inverse_ref)

    pl.semaphore_wait(barrier, len(greeted))
    cotangent_copy = remote(
        cotangent_hbm.at[pl.ds(ROWS, 2 * BLOCK)], received_ref, cotangent_sem.at[0], cotangent_sem.at[1],
        (lax.rem(dp + n_dp - 1, n_dp), x),
    )
    cotangent_copy.start()

    for load in weight_loads + loads[1:]:
        load.wait()

    def forward(head, carry):
        project(head, normed_b_ref, weight_ref, acts_ref, slope_ref)
        attend(head, acts_ref, table_ref, length_ref, first_ref, weights_ref, factor_ref, attended_ref)
        return carry

    lax.fori_loop(0, HEADS, forward, 0)

    cotangent_copy.wait_recv()
    take_upstream(own_ref, received_ref, slot_ref, length_ref, first_ref, upstream_ref)
    mix_back(upstream_ref, out_weight_ref, d_mixed_ref)
    mix(acts_ref, attended_ref, d_mixed_ref, slope_ref, mixed_ref, d_attended_ref, d_proj_ref)

    def put_term(s, value):
        term[s] = value.astype(BF16).reshape(4, 4, 2, 16, D)

    def core_copy(s):
        return remote(
            term.at[s, :, :, other], core_in.at[s], core_sem.at[0, s], core_sem.at[1, s],
            device(x, y, z, other),
        )

    def x_copy(s, k):
        return remote(
            x_out.at[s, x_peer(k)], x_in.at[s, k - 1], x_sem.at[0, s, k - 1], x_sem.at[1, s, k - 1],
            device(x_peer(k), y, z, core),
        )

    def after_core(s):
        core_copy(s).wait_recv()

        def body(g, carry):
            for zz in range(4):
                both = term[s, g, zz, core].astype(F32) + core_in[s, g, zz].astype(F32)
                both = both.astype(BF16)
                for k in range(NX):
                    x_out[s, k, g, zz] = both[:, k * 128 : (k + 1) * 128]
            return carry

        lax.fori_loop(0, 4, body, 0)
        for k in (2, 1, 3):
            x_copy(s, k).start()

    def after_x(s):
        for k in range(1, NX):
            x_copy(s, k).wait_recv()

        def body(g, carry):
            total = x_out[s, x, g].astype(F32)
            for k in range(NX - 1):
                total = total + x_in[s, k, g].astype(F32)
            x_sum[s, g] = total.astype(BF16)
            return carry

        lax.fori_loop(0, 4, body, 0)

    def y_copy(h, g):
        to_y = 2 * g + lax.div(h, 2)
        slot = lax.rem(lax.rem(y - to_y + NY - 1, NY), NY - 1)
        return to_y != y, remote(
            x_sum.at[1 + h, g],
            y_in.at[lax.rem(h, 2), slot],
            y_send.at[h, g],
            y_recv.at[lax.rem(h, 2), slot],
            device(x, to_y, z, core),
        )

    def y_start(h):
        for g in range(4):
            away, copy = y_copy(h, g)
            pl.when(away)(copy.start)

    def after_y(h):
        @pl.when(lax.rem(y, 2) == lax.div(h, 2))
        def _():
            half = lax.rem(h, 2)
            for k in range(NY - 1):
                remote(
                    x_sum.at[1 + h, 0], y_in.at[half, k], y_send.at[h, 0], y_recv.at[half, k],
                    device(x, y_peer(1), z, core),
                ).wait_recv()
            total = x_sum[1 + h, lax.div(y, 2)].astype(F32)
            for k in range(NY - 1):
                total = total + y_in[half, k].astype(F32)
            y_sum[half] = total.astype(BF16)

    def out_chunk(ref, at_y, *lead):
        return ref.at[(*lead, lax.div(at_y, 2), pl.ds(lax.rem(at_y, 2) * 2, 2))]

    def out_y_copy(k):
        return remote(
            out_chunk(x_sum, y_peer(k), 0), out_y_in.at[k - 1], out_y_sem.at[0, k - 1],
            out_y_sem.at[1, k - 1], device(x, y_peer(k), z, core),
        )

    def out_z_copy(k):
        return remote(
            out_z_all.at[z], out_z_all.at[z], out_z_sem.at[0, k - 1], out_z_sem.at[1, k - 1],
            device(x, y, z_peer(k), core),
        )

    def out_y_back_copy(k):
        return remote(
            out_chunk(out_mine, y), out_chunk(out_mine, y), out_y_back_sem.at[0, k - 1],
            out_y_back_sem.at[1, k - 1], device(x, y_peer(k), z, core),
        )

    def out_x_back_copy(k):
        return remote(
            out_mine, out_x_all.at[x], out_x_back_sem.at[0, k - 1], out_x_back_sem.at[1, k - 1],
            device(x_peer(k), y, z, core),
        )

    out_core_back_copy = remote(
        out_x_all, out_core_in, out_core_back_sem.at[0], out_core_back_sem.at[1], device(x, y, z, other)
    )

    def out_y_start():
        for k in range(1, NY):
            out_y_copy(k).start()

    def out_after_y():
        for k in range(1, NY):
            out_y_copy(k).wait_recv()
        total = out_chunk(x_sum, y, 0)[...].astype(F32)
        for k in range(NY - 1):
            total = total + out_y_in[k].astype(F32)
        out_z_all[z] = total.astype(BF16)
        for k in range(1, NZ):
            out_z_copy(k).start()

    def out_after_z():
        for k in range(1, NZ):
            out_z_copy(k).wait_recv()
        total = out_z_all[0].astype(F32)
        for k in range(1, NZ):
            total = total + out_z_all[k].astype(F32)
        out_chunk(out_mine, y)[...] = total.astype(BF16)
        for k in range(1, NY):
            out_y_back_copy(k).start()

    def out_after_y_back():
        for k in range(1, NY):
            out_y_back_copy(k).wait_recv()
        out_x_all[x] = out_mine[...]
        for k in range(1, NX):
            out_x_back_copy(k).start()

    def out_after_x_back():
        for k in range(1, NX):
            out_x_back_copy(k).wait_recv()
        out_core_back_copy.start()

    def out_finish():
        out_core_back_copy.wait_recv()
        for from_core, gathered in ((core, out_x_all), (other, out_core_in)):
            for g in range(4):
                for zz in range(4):
                    at = pl.multiple_of(g * 128 + zz * 32 + from_core * 16, 16)
                    for k in range(NX):
                        out_grad_ref[pl.ds(at, 16), k * 128 : (k + 1) * 128] = gathered[k, g, zz]

    bias_steps = (
        (bias_core, bias_core_sem, core, 2, lambda k: device(x, y, z, other)),
        (bias_x, bias_x_sem, x, NX, lambda k: device(x_peer(k), y, z, core)),
        (bias_y, bias_y_sem, y, NY, lambda k: device(x, y_peer(k), z, core)),
        (bias_z, bias_z_sem, z, NZ, lambda k: device(x, y, z_peer(k), core)),
    )

    def bias_copies(step):
        buffer, sems, at, count, peer = bias_steps[step]
        return [
            remote(buffer.at[at], buffer.at[at], sems.at[0, k - 1], sems.at[1, k - 1], peer(k))
            for k in range(1, count)
        ]

    def bias_start(step, value):
        bias_steps[step][0][bias_steps[step][2]] = value
        for copy in bias_copies(step):
            copy.start()

    def bias_finish(step):
        for copy in bias_copies(step):
            copy.wait_recv()
        buffer, count = bias_steps[step][0], bias_steps[step][3]
        total = buffer[0]
        for k in range(1, count):
            total = total + buffer[k]
        return total

    put_term(0, dot_left_t(mixed_ref[...], upstream_ref[...]))
    core_copy(0).start()
    bias_grad_ref[...] = jnp.zeros_like(bias_grad_ref)

    def backward(head, carry):
        attend_back(
            head, acts_ref, weights_ref, factor_ref, d_attended_ref, slope_ref, d_logits_ref, d_proj_ref,
            bias_grad_ref,
        )
        after_core(head)

        @pl.when(head >= 1)
        def _():
            after_x(head - 1)

        pl.when(head == 1)(out_y_start)

        @pl.when(head >= 2)
        def _():
            y_start(head - 2)

        pl.when(head == 2)(out_after_y)

        @pl.when(head == 3)
        def _():
            after_y(0)
            out_after_z()

        put_term(1 + head, dot_left_t(d_proj_ref[head], normed_b_ref[...]))
        core_copy(1 + head).start()
        return carry

    lax.fori_loop(0, HEADS, backward, 0)

    bias_start(0, bias_grad_ref[...])
    token_grads(0, d_proj_ref, weight_ref, normed_ref, inverse_ref, upstream_ref, token_grad_ref)
    after_core(4)
    bias_start(1, bias_finish(0))
    after_x(3)
    y_start(2)
    after_y(1)
    out_after_y_back()
    token_grads(1, d_proj_ref, weight_ref, normed_ref, inverse_ref, upstream_ref, token_grad_ref)
    after_x(4)
    y_start(3)
    bias_start(2, bias_finish(1))
    after_y(2)
    out_after_x_back()
    after_y(3)

    def z_copy(k):
        to_z = z_peer(k)
        return remote(
            y_sum.at[lax.div(to_z, 4), lax.rem(to_z, 4)], z_in.at[k - 1], z_sem.at[0, k - 1],
            z_sem.at[1, k - 1], device(x, y, to_z, core),
        )

    for k in range(1, NZ):
        z_copy(k).start()
    bias_start(3, bias_finish(2))
    out_finish()
    for k in range(1, NZ):
        z_copy(k).wait_recv()
    total = y_sum[lax.div(z, 4), lax.rem(z, 4)].astype(F32)
    for k in range(NZ - 1):
        total = total + z_in[k].astype(F32)
    column_sum[...] = total

    def column_copy(k):
        return remote(
            column_sum, column_in.at[k - 1], column_sem.at[0, k - 1], column_sem.at[1, k - 1],
            device(x_peer(k), y, z, core),
        )

    for k in range(1, NX):
        column_copy(k).start()
    bias_grad_ref[...] = bias_finish(3)

    for k in range(1, NX):
        column_copy(k).wait_recv()
    for k in range(NX):
        part = column_sum[...] if k == 0 else column_in[k - 1]
        mine = part[0:4]
        for at in range(1, NX):
            mine = jnp.where(jnp.full((4, 128), x, jnp.int32) == at, part[4 * at : 4 * at + 4], mine)
        from_x = lax.rem(x + NX - k, NX)
        proj_grad_ref[:, pl.ds(pl.multiple_of(from_x * 128, 128), 128)] = mine

    cotangent_copy.wait_send()
    for s in range(SETS):
        core_copy(s).wait_send()
        for k in range(1, NX):
            x_copy(s, k).wait_send()
    for h in range(HEADS):
        for g in range(4):
            away, copy = y_copy(h, g)
            pl.when(away)(copy.wait_send)
    for k in range(1, NY):
        out_y_copy(k).wait_send()
        out_y_back_copy(k).wait_send()
    for k in range(1, NZ):
        out_z_copy(k).wait_send()
        z_copy(k).wait_send()
    for k in range(1, NX):
        out_x_back_copy(k).wait_send()
        column_copy(k).wait_send()
    out_core_back_copy.wait_send()
    for step in range(4):
        for copy in bias_copies(step):
            copy.wait_send()


DMA = pltpu.SemaphoreType.DMA
ARGUMENT_SCRATCH = [
    pltpu.VMEM((ROWS, D), BF16),
    pltpu.VMEM((ROWS, D), BF16),
    pltpu.VMEM((2 * BLOCK, D), BF16),
    pltpu.VMEM((HEADS, D, D), BF16),
    pltpu.VMEM((D, D), BF16),
    pltpu.SMEM((HEADS, BUCKETS), F32),
    pltpu.SMEM((BLOCKS,), jnp.int32),
    pltpu.SMEM((BLOCKS,), jnp.int32),
    pltpu.SMEM((BLOCKS,), jnp.int32),
]
LAYER_SCRATCH = [
    pltpu.VMEM((ROWS, D), F32),
    pltpu.VMEM((ROWS, D), BF16),
    pltpu.VMEM((ROWS, BLOCK), F32),
    pltpu.VMEM((HEADS, ROWS, D), BF16),
    pltpu.VMEM((HEADS, ROWS, D), F32),
    pltpu.VMEM((ROWS, D), BF16),
    pltpu.VMEM((HEADS, ROWS, 128), F32),
    pltpu.VMEM((HEADS, ROWS, ROWS), BF16),
    pltpu.VMEM((HEADS, ROWS, ROWS), F32),
    pltpu.VMEM((HEADS, ROWS, 128), F32),
    pltpu.VMEM((ROWS, D), BF16),
    pltpu.VMEM((HEADS, ROWS, 128), BF16),
    pltpu.VMEM((ROWS, ROWS), BF16),
    pltpu.VMEM((HEADS, ROWS, D), BF16),
]
SUM_SCRATCH = [
    pltpu.VMEM((SETS, 4, 4, 2, 16, D), BF16),
    pltpu.VMEM((SETS, 4, 4, 16, D), BF16),
    pltpu.VMEM((SETS, NX, 4, 4, 16, 128), BF16),
    pltpu.VMEM((SETS, NX - 1, 4, 4, 16, 128), BF16),
    pltpu.VMEM((SETS, 4, 4, 16, 128), BF16),
    pltpu.VMEM((2, NY - 1, 4, 16, 128), BF16),
    pltpu.VMEM((2, 4, 16, 128), BF16),
    pltpu.VMEM((NZ - 1, 16, 128), BF16),
    pltpu.VMEM((16, 128), F32),
    pltpu.VMEM((NX - 1, 16, 128), F32),
    pltpu.VMEM((NY - 1, 2, 16, 128), BF16),
    pltpu.VMEM((NZ, 2, 16, 128), BF16),
    pltpu.VMEM((4, 4, 16, 128), BF16),
    pltpu.VMEM((NX, 4, 4, 16, 128), BF16),
    pltpu.VMEM((NX, 4, 4, 16, 128), BF16),
    pltpu.VMEM((2, 8, 128), F32),
    pltpu.VMEM((NX, 8, 128), F32),
    pltpu.VMEM((NY, 8, 128), F32),
    pltpu.VMEM((NZ, 8, 128), F32),
]
SEMAPHORES = [
    DMA((23,)),
    DMA((2,)),
    DMA((2, SETS)),
    DMA((2, SETS, NX - 1)),
    DMA((HEADS, 4)),
    DMA((2, NY - 1)),
    DMA((2, NZ - 1)),
    DMA((2, NX - 1)),
    DMA((2, NY - 1)),
    DMA((2, NZ - 1)),
    DMA((2, NY - 1)),
    DMA((2, NX - 1)),
    DMA((2,)),
    DMA((2, 1)),
    DMA((2, NX - 1)),
    DMA((2, NY - 1)),
    DMA((2, NZ - 1)),
]


def shards(tokens, cotangent, weight, out_weight, table, length, first, slot):
    vmem = pl.BlockSpec(memory_space=pltpu.VMEM)
    token_grad, proj_grad, out_grad, bias_grad = pl.pallas_call(
        layer_kernel,
        out_shape=(
            jax.ShapeDtypeStruct((ROWS, D), BF16),
            jax.ShapeDtypeStruct((4, D), F32),
            jax.ShapeDtypeStruct((D, D), BF16),
            jax.ShapeDtypeStruct((8, 128), F32),
        ),
        in_specs=[pl.BlockSpec(memory_space=pl.ANY)] * 8,
        out_specs=(vmem,) * 4,
        scratch_shapes=ARGUMENT_SCRATCH + LAYER_SCRATCH + SUM_SCRATCH + SEMAPHORES,
        compiler_params=pltpu.CompilerParams(
            vmem_limit_bytes=52 * 2**20, collective_id=0, has_side_effects=True
        ),
        name="layer_grads",
    )(tokens, cotangent, weight, out_weight, table, length, first, slot)
    return token_grad, proj_grad.T, out_grad.astype(F32), bias_grad[:HEADS, :BUCKETS]


def solution(mesh):
    split = P(("dp", "rep"))
    return jax.shard_map(
        shards,
        mesh=mesh,
        in_specs=(split, split, P(), P(), P(), split, split, split),
        out_specs=(split, P(None, ("dp", "rep")), P(), P()),
        check_vma=False,
    )
```

```python
import jax
import jax.numpy as jnp
from jax import lax
from jax.experimental import pallas as pl
from jax.experimental.pallas import tpu as pltpu
from jax.sharding import PartitionSpec as P

HEADS = 4
HEAD_DIM = 128
BLOCK = 128
BLOCKS = 4
SLOTS = 6
BUCKETS = 10
NX, NY, NZ = 4, 8, 8
SETS = HEADS + 2
D = 512
ROWS = BLOCKS * BLOCK
EPSILON = 1e-06
SCALE = HEAD_DIM ** (-0.5)
BF16 = jnp.bfloat16
F32 = jnp.float32
GATE, VALUE, QUERY, KEY = (slice(g * 128, (g + 1) * 128) for g in range(4))
BUCKETS_AT = (range(0, 8), range(1, 9), range(8, 10), range(9, 10))


def dot(a, b):
    return lax.dot_general(a, b, (((1,), (0,)), ((), ())), preferred_element_type=F32)


def dot_right_t(a, b):
    return lax.dot_general(a, b, (((1,), (1,)), ((), ())), preferred_element_type=F32)


def dot_left_t(a, b):
    return lax.dot_general(a, b, (((0,), (0,)), ((), ())), preferred_element_type=F32)


def row_sum(parts):
    total = parts[0]
    for part in parts[1:]:
        total = total + part
    return jnp.sum(total, axis=-1, keepdims=True)


def tile_iota(axis):
    return lax.broadcasted_iota(jnp.int32, (BLOCK, BLOCK), axis)


def norm_tokens(tokens_ref, normed_ref, normed_b_ref, inverse_ref):
    def body(b, carry):
        rows = pl.ds(pl.multiple_of(b * BLOCK, BLOCK), BLOCK)
        x = tokens_ref[rows, :].astype(F32)
        centered = x - jnp.mean(x, axis=-1, keepdims=True)
        inverse = lax.rsqrt(jnp.mean(centered * centered, axis=-1, keepdims=True) + EPSILON)
        normed = centered * inverse
        normed_ref[rows, :] = normed
        normed_b_ref[rows, :] = normed.astype(BF16)
        inverse_ref[rows, :] = jnp.broadcast_to(inverse, (BLOCK, BLOCK))
        return carry

    lax.fori_loop(0, BLOCKS, body, 0)


def project(head, normed_b_ref, weight_ref, acts_ref, slope_ref):
    for c in range(2):
        lanes = pl.ds(c * 256, 256)
        half = dot(normed_b_ref[...], weight_ref[head, :, lanes]) * 0.5
        u = 1.0 + jnp.tanh(half)
        act = half * u
        slope_ref[head, :, lanes] = 0.5 * (u + act * (2.0 - u))
        acts_ref[head, :, lanes] = act.astype(BF16)


def take_upstream(own_ref, received_ref, slot_ref, length_ref, first_ref, upstream_ref):
    def body(b, carry):
        rows = pl.ds(pl.multiple_of(b * BLOCK, BLOCK), BLOCK)
        slot = jnp.full((BLOCK, D), lax.rem(slot_ref[b], SLOTS), jnp.int32)
        value = own_ref[0:BLOCK, :].astype(F32)
        for at in range(1, SLOTS):
            ref, row_at = (own_ref, at * BLOCK) if at < BLOCKS else (received_ref, (at - BLOCKS) * BLOCK)
            value = jnp.where(slot == at, ref[row_at : row_at + BLOCK, :].astype(F32), value)
        limit = length_ref[b] - (b - first_ref[b]) * BLOCK
        row = lax.broadcasted_iota(jnp.int32, (BLOCK, D), 0)
        value = jnp.where(row < limit, value, 0.0)
        upstream_ref[rows, :] = value.astype(BF16)
        return carry

    lax.fori_loop(0, BLOCKS, body, 0)


def mix_back(upstream_ref, out_weight_ref, d_mixed_ref):
    for c in range(2):
        part = dot_right_t(upstream_ref[...], out_weight_ref[c * 256 : (c + 1) * 256, :])
        for k in range(2):
            d_mixed_ref[2 * c + k] = part[:, k * 128 : (k + 1) * 128]


def bucket_bounds(apart):
    distance = tile_iota(0) - tile_iota(1) + apart * BLOCK
    return distance, [(bucket, 0 if bucket == 0 else 2 ** (bucket - 1)) for bucket in BUCKETS_AT[apart]]


def bias_tiles(table_ref, head):
    tiles = []
    for apart in range(BLOCKS):
        distance, bounds = bucket_bounds(apart)
        tile = jnp.full((BLOCK, BLOCK), table_ref[head, bounds[0][0]] * 0.5, F32)
        for bucket, least in bounds[1:]:
            tile = jnp.where(distance >= least, table_ref[head, bucket] * 0.5, tile)
        tiles.append(tile)
    return tiles


def attend(head, acts_ref, table_ref, length_ref, first_ref, weights_ref, factor_ref, attended_ref):
    bias = bias_tiles(table_ref, head)
    row = tile_iota(0)
    causal_row = jnp.where(tile_iota(1) <= row, row, ROWS)
    for i in range(BLOCKS):
        rows = pl.ds(i * BLOCK, BLOCK)
        upto = (i + 1) * BLOCK
        scores = dot_right_t(acts_ref[head, rows, QUERY], acts_ref[head, 0:upto, KEY])
        for j in range(i + 1):
            lanes = pl.ds(j * BLOCK, BLOCK)
            limit = jnp.where(
                first_ref[i] == first_ref[j], length_ref[i] - (i - first_ref[i]) * BLOCK, 0
            )
            half = scores[:, j * BLOCK : (j + 1) * BLOCK] * (0.5 * SCALE) + bias[i - j]
            kept = (causal_row if i == j else row) < limit
            u = jnp.where(kept, 1.0 + jnp.tanh(half), 0.0)
            weight = half * u
            factor_ref[head, rows, lanes] = 0.5 * (u + weight * (2.0 - u))
            weights_ref[head, rows, lanes] = weight.astype(BF16)
        attended_ref[head, rows, :] = dot(
            weights_ref[head, rows, 0:upto], acts_ref[head, 0:upto, VALUE]
        )


def mix(acts_ref, attended_ref, d_mixed_ref, slope_ref, mixed_ref, d_attended_ref, d_proj_ref):
    def body(b, carry):
        rows = pl.ds(pl.multiple_of(b * BLOCK, BLOCK), BLOCK)
        heads = range(HEADS)
        att = [attended_ref[h, rows, :] for h in heads]
        mean = row_sum(att) * (1.0 / D)
        centered = [a - mean for a in att]
        inverse = lax.rsqrt(row_sum([c * c for c in centered]) * (1.0 / D) + EPSILON)
        normed = [c * inverse for c in centered]
        gate = [acts_ref[h, rows, GATE].astype(F32) for h in heads]
        d_mixed = [d_mixed_ref[h, rows, :] for h in heads]
        g = [d_mixed[h] * gate[h] for h in heads]
        g_mean = row_sum(g) * (1.0 / D)
        g_dot = row_sum([g[h] * normed[h] for h in heads]) * (1.0 / D)
        for h in heads:
            mixed_ref[rows, pl.ds(h * 128, 128)] = (normed[h] * gate[h]).astype(BF16)
            d_attended_ref[h, rows, :] = (inverse * (g[h] - g_mean - normed[h] * g_dot)).astype(BF16)
            d_proj_ref[h, rows, GATE] = (d_mixed[h] * normed[h] * slope_ref[h, rows, GATE]).astype(BF16)
        return carry

    lax.fori_loop(0, BLOCKS, body, 0)


def attend_back(
    head, acts_ref, weights_ref, factor_ref, d_attended_ref, slope_ref, d_logits_ref, d_proj_ref, bias_ref
):
    sums = [None] * BLOCKS
    for i in range(BLOCKS):
        rows = pl.ds(i * BLOCK, BLOCK)
        upto = (i + 1) * BLOCK
        d_weights = dot_right_t(d_attended_ref[head, rows, :], acts_ref[head, 0:upto, VALUE])
        for j in range(i + 1):
            lanes = pl.ds(j * BLOCK, BLOCK)
            d_logits = d_weights[:, j * BLOCK : (j + 1) * BLOCK] * factor_ref[head, rows, lanes]
            sums[i - j] = d_logits if sums[i - j] is None else sums[i - j] + d_logits
            d_logits_ref[rows, lanes] = d_logits.astype(BF16)
        d_query = dot(d_logits_ref[rows, 0:upto], acts_ref[head, 0:upto, KEY])
        d_proj_ref[head, rows, QUERY] = (d_query * SCALE * slope_ref[head, rows, QUERY]).astype(BF16)
    for j in range(BLOCKS):
        rows = pl.ds(j * BLOCK, BLOCK)
        below = pl.ds(j * BLOCK, ROWS - j * BLOCK)
        d_value = dot_left_t(weights_ref[head, below, rows], d_attended_ref[head, below, :])
        d_proj_ref[head, rows, VALUE] = (d_value * slope_ref[head, rows, VALUE]).astype(BF16)
        d_key = dot_left_t(d_logits_ref[below, rows], acts_ref[head, below, QUERY])
        d_proj_ref[head, rows, KEY] = (d_key * SCALE * slope_ref[head, rows, KEY]).astype(BF16)
    totals = [None] * BUCKETS
    for apart in range(BLOCKS):
        distance, bounds = bucket_bounds(apart)
        for at, (bucket, least) in enumerate(bounds):
            value = sums[apart]
            if at > 0:
                value = jnp.where(distance >= least, value, 0.0)
            if at + 1 < len(bounds):
                value = jnp.where(distance < bounds[at + 1][1], value, 0.0)
            value = jnp.sum(value, axis=0, keepdims=True)
            totals[bucket] = value if totals[bucket] is None else totals[bucket] + value
    lane = lax.broadcasted_iota(jnp.int32, (1, 128), 1)
    packed = jnp.zeros((1, 128), F32)
    for bucket in range(BUCKETS):
        packed = jnp.where(lane == bucket, jnp.sum(totals[bucket], axis=1, keepdims=True), packed)
    bias_ref[pl.ds(head, 1), :] = packed


def token_grads(part, d_proj_ref, weight_ref, normed_ref, inverse_ref, upstream_ref, token_grad_ref):
    rows = pl.ds(part * 256, 256)
    d_normed = dot_right_t(d_proj_ref[0, rows, :], weight_ref[0])
    for h in range(1, HEADS):
        d_normed = d_normed + dot_right_t(d_proj_ref[h, rows, :], weight_ref[h])
    normed = normed_ref[rows, :]
    inverse = inverse_ref[rows, 0:1]
    mean = jnp.mean(d_normed, axis=-1, keepdims=True)
    along = jnp.mean(d_normed * normed, axis=-1, keepdims=True)
    back = inverse * (d_normed - mean - normed * along)
    token_grad_ref[rows, :] = (upstream_ref[rows, :].astype(F32) + back).astype(BF16)


def place():
    dp = lax.axis_index("dp")
    return lax.axis_index("rep"), lax.div(dp, 2 * NZ), lax.rem(lax.div(dp, 2), NZ), lax.rem(dp, 2)


def device(x, y, z, core):
    return ((y * NZ + z) * 2 + core, x)


def layer_kernel(
    tokens_hbm, cotangent_hbm, weight_hbm, out_weight_hbm, table_hbm, length_hbm, first_hbm, slot_hbm,
    token_grad_ref, proj_grad_ref, out_grad_ref, bias_grad_ref,
    tokens_ref, own_ref, received_ref, weight_ref, out_weight_ref, table_ref, length_ref, first_ref, slot_ref,
    normed_ref, normed_b_ref, inverse_ref, acts_ref, slope_ref, upstream_ref, d_mixed_ref, weights_ref,
    factor_ref, attended_ref, mixed_ref, d_attended_ref, d_logits_ref, d_proj_ref,
    term, core_in, x_out, x_in, x_sum, y_in, y_sum, z_in,
    out_y_in, out_z_all, out_mine, out_x_all, out_core_in,
    bias_core, bias_x, bias_y, bias_z,
    load_sem, cotangent_sem, core_sem, x_sem, y_send, y_recv, z_sem,
    out_y_sem, out_z_sem, out_y_back_sem, out_x_back_sem, out_core_back_sem,
    bias_core_sem, bias_x_sem, bias_y_sem, bias_z_sem,
):
    x, y, z, core = place()
    other = 1 - core
    dp = lax.axis_index("dp")
    n_dp = 2 * NY * NZ

    def x_peer(k):
        return lax.rem(x + k, NX)

    def y_peer(k):
        return lax.rem(y + k, NY)

    def z_peer(k):
        return lax.rem(z + k, NZ)

    def remote(src, dst, send, recv, target):
        return pltpu.make_async_remote_copy(
            src_ref=src, dst_ref=dst, send_sem=send, recv_sem=recv, device_id=target,
            device_id_type=pl.DeviceIdType.MESH,
        )

    loads = [
        pltpu.make_async_copy(tokens_hbm, tokens_ref, load_sem.at[0]),
        pltpu.make_async_copy(table_hbm, table_ref, load_sem.at[1]),
        pltpu.make_async_copy(length_hbm, length_ref, load_sem.at[2]),
        pltpu.make_async_copy(first_hbm, first_ref, load_sem.at[3]),
        pltpu.make_async_copy(slot_hbm, slot_ref, load_sem.at[4]),
        pltpu.make_async_copy(cotangent_hbm.at[pl.ds(0, ROWS)], own_ref, load_sem.at[5]),
        pltpu.make_async_copy(out_weight_hbm, out_weight_ref, load_sem.at[6]),
    ]

    def weight_load(h, g):
        return pltpu.make_async_copy(
            weight_hbm.at[:, pl.ds(pl.multiple_of(g * D + h * 128, 128), 128)],
            weight_ref.at[h, :, pl.ds(g * 128, 128)],
            load_sem.at[7 + h * 4 + g],
        )

    weight_loads = [weight_load(h, g) for h in range(HEADS) for g in range(4)]
    for load in loads[:1] + weight_loads + loads[1:]:
        load.start()

    barrier = pltpu.get_barrier_semaphore()
    greeted = [device(x, y, z, other)]
    greeted += [device(x_peer(k), y, z, core) for k in range(1, NX)]
    greeted += [device(x, y_peer(k), z, core) for k in range(1, NY)]
    greeted += [device(x, y, z_peer(k), core) for k in range(1, NZ)]
    greeted += [(lax.rem(dp + n_dp + 2 * core - 1, n_dp), x)]
    for target in greeted:
        pl.semaphore_signal(barrier, inc=1, device_id=target, device_id_type=pl.DeviceIdType.MESH)

    loads[0].wait()
    norm_tokens(tokens_ref, normed_ref, normed_b_ref, inverse_ref)

    pl.semaphore_wait(barrier, len(greeted))
    cotangent_copy = remote(
        cotangent_hbm.at[pl.ds(ROWS, 2 * BLOCK)], received_ref, cotangent_sem.at[0], cotangent_sem.at[1],
        (lax.rem(dp + n_dp - 1, n_dp), x),
    )
    cotangent_copy.start()

    for load in loads[1:5]:
        load.wait()

    def forward(head, carry):
        for g in range(4):
            weight_load(head, g).wait()
        project(head, normed_b_ref, weight_ref, acts_ref, slope_ref)
        attend(head, acts_ref, table_ref, length_ref, first_ref, weights_ref, factor_ref, attended_ref)
        return carry

    lax.fori_loop(0, HEADS, forward, 0)

    for load in loads[5:]:
        load.wait()
    cotangent_copy.wait_recv()
    take_upstream(own_ref, received_ref, slot_ref, length_ref, first_ref, upstream_ref)
    mix_back(upstream_ref, out_weight_ref, d_mixed_ref)
    mix(acts_ref, attended_ref, d_mixed_ref, slope_ref, mixed_ref, d_attended_ref, d_proj_ref)

    def put_term(s, value):
        units = value.shape[0] // 128
        term[s, 0:units] = value.astype(BF16).reshape(units, 4, 2, 16, D)

    def units_of(s):
        return pl.ds(0, 4 if s < 2 else 3)

    def core_copy(s):
        return remote(
            term.at[s, units_of(s), :, other], core_in.at[s, units_of(s)], core_sem.at[0, s], core_sem.at[1, s],
            device(x, y, z, other),
        )

    def x_copy(s, k):
        return remote(
            x_out.at[s, x_peer(k), units_of(s)], x_in.at[s, k - 1, units_of(s)], x_sem.at[0, s, k - 1], x_sem.at[1, s, k - 1],
            device(x_peer(k), y, z, core),
        )

    def by_lanes(both):
        return [both[:, k * 128 : (k + 1) * 128] for k in range(NX)]

    def by_columns(both):
        upper = lax.broadcasted_iota(jnp.int32, (8, 128), 0) < 4
        parts = []
        for k in range(NX):
            rows = both[(k // 2) * 8 : (k // 2) * 8 + 8]
            quarters = [rows[:, q * 128 : (q + 1) * 128] for q in range(4)]
            if k % 2 == 0:
                pairs = [jnp.where(upper, quarters[q], pltpu.roll(quarters[q + 1], 4, 0)) for q in (0, 2)]
            else:
                pairs = [jnp.where(upper, pltpu.roll(quarters[q], 4, 0), quarters[q + 1]) for q in (0, 2)]
            parts.append(jnp.concatenate(pairs, axis=0))
        return parts

    def after_core(s):
        core_copy(s).wait_recv()

        def body(g, carry):
            for zz in range(4):
                both = term[s, g, zz, core].astype(F32) + core_in[s, g, zz].astype(F32)
                for k, part in enumerate(by_lanes(both) if s == 0 else by_columns(both)):
                    x_out[s, k, g, zz] = part.astype(BF16)
            return carry

        lax.fori_loop(0, 4 if s < 2 else 3, body, 0)
        for k in (2, 1, 3):
            x_copy(s, k).start()

    def after_x(s):
        for k in range(1, NX):
            x_copy(s, k).wait_recv()
        for g in range(4 if s < 2 else 3):
            total = x_out[s, x, g].astype(F32)
            for k in range(NX - 1):
                total = total + x_in[s, k, g].astype(F32)
            x_sum[s, g] = total.astype(BF16)

    def y_copy(g, h):
        to_y = 2 * g + h // 2
        slot = lax.rem(lax.rem(y - to_y + NY - 1, NY), NY - 1)
        return to_y != y, remote(
            x_sum.at[1, h] if g == 0 else x_sum.at[2 + h, g - 1],
            y_in.at[h % 2, slot],
            y_send.at[g, h],
            y_recv.at[h % 2, slot],
            device(x, to_y, z, core),
        )

    def y_start(units):
        for g, h in units:
            away, copy = y_copy(g, h)
            pl.when(away)(copy.start)

    def add_y(half, own):
        for k in range(NY - 1):
            remote(
                x_sum.at[1, 0], y_in.at[half, k], y_send.at[0, 0], y_recv.at[half, k],
                device(x, y_peer(1), z, core),
            ).wait_recv()
        total = own.astype(F32)
        for k in range(NY - 1):
            total = total + y_in[half, k].astype(F32)
        y_sum[half] = total.astype(BF16)

    def after_y_gate():
        @pl.when(y < 2)
        def _():
            for half in range(2):
                add_y(half, x_sum[1, 2 * y + half])

    def after_y(h):
        @pl.when((y >= 2) & (lax.rem(y, 2) == h // 2))
        def _():
            add_y(h % 2, x_sum[2 + h, lax.div(y, 2) - 1])

    def out_chunk(ref, at_y, *lead):
        return ref.at[(*lead, lax.div(at_y, 2), pl.ds(lax.rem(at_y, 2) * 2, 2))]

    def out_y_copy(k):
        return remote(
            out_chunk(x_sum, y_peer(k), 0), out_y_in.at[k - 1], out_y_sem.at[0, k - 1],
            out_y_sem.at[1, k - 1], device(x, y_peer(k), z, core),
        )

    def out_z_copy(k):
        return remote(
            out_z_all.at[z], out_z_all.at[z], out_z_sem.at[0, k - 1], out_z_sem.at[1, k - 1],
            device(x, y, z_peer(k), core),
        )

    def out_y_back_copy(k):
        return remote(
            out_chunk(out_mine, y), out_chunk(out_mine, y), out_y_back_sem.at[0, k - 1],
            out_y_back_sem.at[1, k - 1], device(x, y_peer(k), z, core),
        )

    def out_x_back_copy(k):
        return remote(
            out_mine, out_x_all.at[x], out_x_back_sem.at[0, k - 1], out_x_back_sem.at[1, k - 1],
            device(x_peer(k), y, z, core),
        )

    out_core_back_copy = remote(
        out_x_all, out_core_in, out_core_back_sem.at[0], out_core_back_sem.at[1], device(x, y, z, other)
    )

    def out_y_start():
        for k in range(1, NY):
            out_y_copy(k).start()

    def out_after_y():
        for k in range(1, NY):
            out_y_copy(k).wait_recv()
        total = out_chunk(x_sum, y, 0)[...].astype(F32)
        for k in range(NY - 1):
            total = total + out_y_in[k].astype(F32)
        out_z_all[z] = total.astype(BF16)
        for k in range(1, NZ):
            out_z_copy(k).start()

    def out_after_z():
        for k in range(1, NZ):
            out_z_copy(k).wait_recv()
        total = out_z_all[0].astype(F32)
        for k in range(1, NZ):
            total = total + out_z_all[k].astype(F32)
        out_chunk(out_mine, y)[...] = total.astype(BF16)
        for k in range(1, NY):
            out_y_back_copy(k).start()

    def out_after_y_back():
        for k in range(1, NY):
            out_y_back_copy(k).wait_recv()
        out_x_all[x] = out_mine[...]
        for k in range(1, NX):
            out_x_back_copy(k).start()

    def out_after_x_back():
        for k in range(1, NX):
            out_x_back_copy(k).wait_recv()
        out_core_back_copy.start()

    def out_finish():
        out_core_back_copy.wait_recv()
        for from_core, gathered in ((core, out_x_all), (other, out_core_in)):
            for g in range(4):
                for zz in range(4):
                    at = pl.multiple_of(g * 128 + zz * 32 + from_core * 16, 16)
                    for k in range(NX):
                        out_grad_ref[pl.ds(at, 16), k * 128 : (k + 1) * 128] = gathered[k, g, zz]

    bias_steps = (
        (bias_core, bias_core_sem, core, 2, lambda k: device(x, y, z, other)),
        (bias_x, bias_x_sem, x, NX, lambda k: device(x_peer(k), y, z, core)),
        (bias_y, bias_y_sem, y, NY, lambda k: device(x, y_peer(k), z, core)),
        (bias_z, bias_z_sem, z, NZ, lambda k: device(x, y, z_peer(k), core)),
    )

    def bias_copies(step):
        buffer, sems, at, count, peer = bias_steps[step]
        return [
            remote(buffer.at[at], buffer.at[at], sems.at[0, k - 1], sems.at[1, k - 1], peer(k))
            for k in range(1, count)
        ]

    def bias_start(step, value):
        bias_steps[step][0][bias_steps[step][2]] = value
        for copy in bias_copies(step):
            copy.start()

    def bias_finish(step):
        for copy in bias_copies(step):
            copy.wait_recv()
        buffer, count = bias_steps[step][0], bias_steps[step][3]
        total = buffer[0]
        for k in range(1, count):
            total = total + buffer[k]
        return total

    gate_units = [(0, h) for h in range(HEADS)]

    def head_units(h):
        return [(g, h) for g in range(1, 4)]

    def back(head):
        attend_back(
            head, acts_ref, weights_ref, factor_ref, d_attended_ref, slope_ref, d_logits_ref, d_proj_ref,
            bias_grad_ref,
        )

    def send_head(head):
        put_term(2 + head, dot_left_t(d_proj_ref[head, :, 128:D], normed_b_ref[...]))
        core_copy(2 + head).start()

    def tokens_part(part):
        token_grads(part, d_proj_ref, weight_ref, normed_ref, inverse_ref, upstream_ref, token_grad_ref)

    def z_copy(k):
        to_z = z_peer(k)
        return remote(
            y_sum.at[lax.div(to_z, 4), lax.rem(to_z, 4)], z_in.at[k - 1], z_sem.at[0, k - 1],
            z_sem.at[1, k - 1], device(x, y, to_z, core),
        )

    put_term(0, dot_left_t(mixed_ref[...], upstream_ref[...]))
    core_copy(0).start()
    d_gate = jnp.concatenate([d_proj_ref[h, :, GATE] for h in range(HEADS)], axis=1)
    put_term(1, dot_left_t(d_gate, normed_b_ref[...]))
    core_copy(1).start()
    bias_grad_ref[...] = jnp.zeros_like(bias_grad_ref)
    after_core(0)
    back(0)
    after_core(1)
    send_head(0)
    back(1)
    after_core(2)
    send_head(1)
    back(2)
    after_core(3)
    after_x(0)
    out_y_start()
    send_head(2)
    back(3)
    after_core(4)
    after_x(1)
    y_start(gate_units)
    send_head(3)
    bias_start(0, bias_grad_ref[...])
    tokens_part(0)
    after_core(5)
    bias_start(1, bias_finish(0))
    tokens_part(1)
    after_x(2)
    y_start(head_units(0))
    out_after_y()
    after_x(3)
    y_start(head_units(1))
    after_x(4)
    y_start(head_units(2))
    bias_start(2, bias_finish(1))
    after_x(5)
    y_start(head_units(3))
    out_after_z()
    after_y_gate()
    for h in range(HEADS - 1):
        after_y(h)
    bias_start(3, bias_finish(2))
    out_after_y_back()
    after_y(HEADS - 1)
    for k in range(1, NZ):
        z_copy(k).start()
    out_after_x_back()
    for k in range(1, NZ):
        z_copy(k).wait_recv()
    total = y_sum[lax.div(z, 4), lax.rem(z, 4)].astype(F32)
    for k in range(NZ - 1):
        total = total + z_in[k].astype(F32)
    for q in range(4):
        proj_grad_ref[:, q * 128 : (q + 1) * 128] = total[4 * q : 4 * q + 4]
    bias_grad_ref[...] = bias_finish(3)
    out_finish()

    cotangent_copy.wait_send()
    for s in range(SETS):
        core_copy(s).wait_send()
        for k in range(1, NX):
            x_copy(s, k).wait_send()
    for h in range(HEADS):
        for g in range(4):
            away, copy = y_copy(g, h)
            pl.when(away)(copy.wait_send)
    for k in range(1, NY):
        out_y_copy(k).wait_send()
        out_y_back_copy(k).wait_send()
    for k in range(1, NZ):
        out_z_copy(k).wait_send()
        z_copy(k).wait_send()
    for k in range(1, NX):
        out_x_back_copy(k).wait_send()
    out_core_back_copy.wait_send()
    for step in range(4):
        for copy in bias_copies(step):
            copy.wait_send()


DMA = pltpu.SemaphoreType.DMA
ARGUMENT_SCRATCH = [
    pltpu.VMEM((ROWS, D), BF16),
    pltpu.VMEM((ROWS, D), BF16),
    pltpu.VMEM((2 * BLOCK, D), BF16),
    pltpu.VMEM((HEADS, D, D), BF16),
    pltpu.VMEM((D, D), BF16),
    pltpu.SMEM((HEADS, BUCKETS), F32),
    pltpu.SMEM((BLOCKS,), jnp.int32),
    pltpu.SMEM((BLOCKS,), jnp.int32),
    pltpu.SMEM((BLOCKS,), jnp.int32),
]
LAYER_SCRATCH = [
    pltpu.VMEM((ROWS, D), F32),
    pltpu.VMEM((ROWS, D), BF16),
    pltpu.VMEM((ROWS, BLOCK), F32),
    pltpu.VMEM((HEADS, ROWS, D), BF16),
    pltpu.VMEM((HEADS, ROWS, D), F32),
    pltpu.VMEM((ROWS, D), BF16),
    pltpu.VMEM((HEADS, ROWS, 128), F32),
    pltpu.VMEM((HEADS, ROWS, ROWS), BF16),
    pltpu.VMEM((HEADS, ROWS, ROWS), F32),
    pltpu.VMEM((HEADS, ROWS, 128), F32),
    pltpu.VMEM((ROWS, D), BF16),
    pltpu.VMEM((HEADS, ROWS, 128), BF16),
    pltpu.VMEM((ROWS, ROWS), BF16),
    pltpu.VMEM((HEADS, ROWS, D), BF16),
]
SUM_SCRATCH = [
    pltpu.VMEM((SETS, 4, 4, 2, 16, D), BF16),
    pltpu.VMEM((SETS, 4, 4, 16, D), BF16),
    pltpu.VMEM((SETS, NX, 4, 4, 16, 128), BF16),
    pltpu.VMEM((SETS, NX - 1, 4, 4, 16, 128), BF16),
    pltpu.VMEM((SETS, 4, 4, 16, 128), BF16),
    pltpu.VMEM((2, NY - 1, 4, 16, 128), BF16),
    pltpu.VMEM((2, 4, 16, 128), BF16),
    pltpu.VMEM((NZ - 1, 16, 128), BF16),
    pltpu.VMEM((NY - 1, 2, 16, 128), BF16),
    pltpu.VMEM((NZ, 2, 16, 128), BF16),
    pltpu.VMEM((4, 4, 16, 128), BF16),
    pltpu.VMEM((NX, 4, 4, 16, 128), BF16),
    pltpu.VMEM((NX, 4, 4, 16, 128), BF16),
    pltpu.VMEM((2, 8, 128), F32),
    pltpu.VMEM((NX, 8, 128), F32),
    pltpu.VMEM((NY, 8, 128), F32),
    pltpu.VMEM((NZ, 8, 128), F32),
]
SEMAPHORES = [
    DMA((23,)),
    DMA((2,)),
    DMA((2, SETS)),
    DMA((2, SETS, NX - 1)),
    DMA((HEADS, 4)),
    DMA((2, NY - 1)),
    DMA((2, NZ - 1)),
    DMA((2, NY - 1)),
    DMA((2, NZ - 1)),
    DMA((2, NY - 1)),
    DMA((2, NX - 1)),
    DMA((2,)),
    DMA((2, 1)),
    DMA((2, NX - 1)),
    DMA((2, NY - 1)),
    DMA((2, NZ - 1)),
]


def shards(tokens, cotangent, weight, out_weight, table, length, first, slot):
    vmem = pl.BlockSpec(memory_space=pltpu.VMEM)
    token_grad, proj_grad, out_grad, bias_grad = pl.pallas_call(
        layer_kernel,
        out_shape=(
            jax.ShapeDtypeStruct((ROWS, D), BF16),
            jax.ShapeDtypeStruct((4, D), F32),
            jax.ShapeDtypeStruct((D, D), BF16),
            jax.ShapeDtypeStruct((8, 128), F32),
        ),
        in_specs=[pl.BlockSpec(memory_space=pltpu.HBM)] * 8,
        out_specs=(vmem,) * 4,
        scratch_shapes=ARGUMENT_SCRATCH + LAYER_SCRATCH + SUM_SCRATCH + SEMAPHORES,
        compiler_params=pltpu.CompilerParams(
            vmem_limit_bytes=60 * 2**20, collective_id=0, has_side_effects=True
        ),
        name="layer_grads",
    )(tokens, cotangent, weight, out_weight, table, length, first, slot)
    return token_grad, proj_grad.T, out_grad.astype(F32), bias_grad[:HEADS, :BUCKETS]


def solution(mesh):
    split = P(("dp", "rep"))
    return jax.shard_map(
        shards,
        mesh=mesh,
        in_specs=(split, split, P(), P(), P(), split, split, split),
        out_specs=(split, P(None, ("dp", "rep")), P(), P()),
        check_vma=False,
    )
```

```python
import jax
import jax.numpy as jnp
from jax import lax
from jax.experimental import pallas as pl
from jax.experimental.pallas import tpu as pltpu
from jax.sharding import PartitionSpec as P

HEADS = 4
HEAD_DIM = 128
BLOCK = 128
BLOCKS = 4
SLOTS = 6
BUCKETS = 10
NX, NY, NZ = 4, 8, 8
SETS = HEADS + 2
D = 512
ROWS = BLOCKS * BLOCK
EPSILON = 1e-06
SCALE = HEAD_DIM ** (-0.5)
BF16 = jnp.bfloat16
F32 = jnp.float32
GATE, VALUE, QUERY, KEY = (slice(g * 128, (g + 1) * 128) for g in range(4))
BUCKETS_AT = (range(0, 8), range(1, 9), range(8, 10), range(9, 10))


def dot(a, b):
    return lax.dot_general(a, b, (((1,), (0,)), ((), ())), preferred_element_type=F32)


def dot_right_t(a, b):
    return lax.dot_general(a, b, (((1,), (1,)), ((), ())), preferred_element_type=F32)


def dot_left_t(a, b):
    return lax.dot_general(a, b, (((0,), (0,)), ((), ())), preferred_element_type=F32)


def row_sum(parts):
    total = parts[0]
    for part in parts[1:]:
        total = total + part
    return jnp.sum(total, axis=-1, keepdims=True)


def tile_iota(axis):
    return lax.broadcasted_iota(jnp.int32, (BLOCK, BLOCK), axis)


def norm_tokens(tokens_ref, normed_ref, normed_b_ref, inverse_ref):
    def body(b, carry):
        rows = pl.ds(pl.multiple_of(b * BLOCK, BLOCK), BLOCK)
        x = tokens_ref[rows, :].astype(F32)
        centered = x - jnp.mean(x, axis=-1, keepdims=True)
        inverse = lax.rsqrt(jnp.mean(centered * centered, axis=-1, keepdims=True) + EPSILON)
        normed = centered * inverse
        normed_ref[rows, :] = normed
        normed_b_ref[rows, :] = normed.astype(BF16)
        inverse_ref[rows, :] = jnp.broadcast_to(inverse, (BLOCK, BLOCK))
        return carry

    lax.fori_loop(0, BLOCKS, body, 0)


def head_weight(weight_ref, head, groups):
    parts = [weight_ref[:, pl.ds(pl.multiple_of(g * D + head * 128, 128), 128)] for g in groups]
    return jnp.concatenate(parts, axis=1)


def project(head, normed_b_ref, weight_ref, acts_ref, slope_ref):
    for r in range(2):
        for c in range(2):
            rows, lanes = pl.ds(r * 256, 256), pl.ds(c * 256, 256)
            half = dot(normed_b_ref[rows, :], head_weight(weight_ref, head, (2 * c, 2 * c + 1))) * 0.5
            u = 1.0 + jnp.tanh(half)
            act = half * u
            slope_ref[head, rows, lanes] = 0.5 * (u + act * (2.0 - u))
            acts_ref[head, rows, lanes] = act.astype(BF16)


def take_upstream(own_ref, received_ref, slot_ref, length_ref, first_ref, upstream_ref):
    def body(b, carry):
        rows = pl.ds(pl.multiple_of(b * BLOCK, BLOCK), BLOCK)
        slot = jnp.full((BLOCK, D), lax.rem(slot_ref[b], SLOTS), jnp.int32)
        value = own_ref[0:BLOCK, :].astype(F32)
        for at in range(1, SLOTS):
            ref, row_at = (own_ref, at * BLOCK) if at < BLOCKS else (received_ref, (at - BLOCKS) * BLOCK)
            value = jnp.where(slot == at, ref[row_at : row_at + BLOCK, :].astype(F32), value)
        limit = length_ref[b] - (b - first_ref[b]) * BLOCK
        row = lax.broadcasted_iota(jnp.int32, (BLOCK, D), 0)
        value = jnp.where(row < limit, value, 0.0)
        upstream_ref[rows, :] = value.astype(BF16)
        return carry

    lax.fori_loop(0, BLOCKS, body, 0)


def mix_back(upstream_ref, out_weight_ref, d_mixed_ref):
    for c in range(2):
        part = dot_right_t(upstream_ref[...], out_weight_ref[c * 256 : (c + 1) * 256, :])
        for k in range(2):
            d_mixed_ref[2 * c + k] = part[:, k * 128 : (k + 1) * 128]


def bucket_bounds(apart):
    distance = tile_iota(0) - tile_iota(1) + apart * BLOCK
    return distance, [(bucket, 0 if bucket == 0 else 2 ** (bucket - 1)) for bucket in BUCKETS_AT[apart]]


def tile_rows(i):
    return slice(i * BLOCK, (i + 1) * BLOCK)


def fill_bias(table_ref, bias_tile_ref):
    def body(head, carry):
        for apart in range(BLOCKS):
            distance, bounds = bucket_bounds(apart)
            tile = jnp.full((BLOCK, BLOCK), table_ref[head, bounds[0][0]] * 0.5, F32)
            for bucket, least in bounds[1:]:
                tile = jnp.where(distance >= least, table_ref[head, bucket] * 0.5, tile)
            bias_tile_ref[head, apart] = tile
        return carry

    lax.fori_loop(0, HEADS, body, 0)


def clear_upper(weights_ref, d_logits_ref):
    zero = jnp.zeros((BLOCK, BLOCK), BF16)
    for i in (0, 2):
        d_logits_ref[tile_rows(i), tile_rows(i + 1)] = zero
        for head in range(HEADS):
            weights_ref[head, tile_rows(i), tile_rows(i + 1)] = zero


def attend(head, acts_ref, bias_tile_ref, length_ref, first_ref, weights_ref, factor_ref, attended_ref):
    row = tile_iota(0)
    causal_row = jnp.where(tile_iota(1) <= row, row, ROWS)
    for pair in range(2):
        upto = (pair + 1) * 256
        pair_rows = pl.ds(pair * 256, 256)
        scores = dot_right_t(acts_ref[head, pair_rows, QUERY], acts_ref[head, 0:upto, KEY])
        for i in (2 * pair, 2 * pair + 1):
            at = (i - 2 * pair) * BLOCK
            for j in range(i + 1):
                limit = jnp.where(
                    first_ref[i] == first_ref[j], length_ref[i] - (i - first_ref[i]) * BLOCK, 0
                )
                half = scores[at : at + BLOCK, tile_rows(j)] * (0.5 * SCALE) + bias_tile_ref[head, i - j]
                kept = (causal_row if i == j else row) < limit
                u = jnp.where(kept, 1.0 + jnp.tanh(half), 0.0)
                weight = half * u
                factor_ref[head, tile_rows(i), tile_rows(j)] = 0.5 * (u + weight * (2.0 - u))
                weights_ref[head, tile_rows(i), tile_rows(j)] = weight.astype(BF16)
        attended_ref[head, pair_rows, :] = dot(
            weights_ref[head, pair_rows, 0:upto], acts_ref[head, 0:upto, VALUE]
        )


def mix(acts_ref, attended_ref, d_mixed_ref, slope_ref, mixed_ref, d_attended_ref, d_proj_ref):
    def body(b, carry):
        rows = pl.ds(pl.multiple_of(b * BLOCK, BLOCK), BLOCK)
        heads = range(HEADS)
        att = [attended_ref[h, rows, :] for h in heads]
        mean = row_sum(att) * (1.0 / D)
        centered = [a - mean for a in att]
        inverse = lax.rsqrt(row_sum([c * c for c in centered]) * (1.0 / D) + EPSILON)
        normed = [c * inverse for c in centered]
        gate = [acts_ref[h, rows, GATE].astype(F32) for h in heads]
        d_mixed = [d_mixed_ref[h, rows, :] for h in heads]
        g = [d_mixed[h] * gate[h] for h in heads]
        g_mean = row_sum(g) * (1.0 / D)
        g_dot = row_sum([g[h] * normed[h] for h in heads]) * (1.0 / D)
        for h in heads:
            mixed_ref[rows, pl.ds(h * 128, 128)] = (normed[h] * gate[h]).astype(BF16)
            d_attended_ref[h, rows, :] = (inverse * (g[h] - g_mean - normed[h] * g_dot)).astype(BF16)
            d_proj_ref[h, rows, GATE] = (d_mixed[h] * normed[h] * slope_ref[h, rows, GATE]).astype(BF16)
        return carry

    lax.fori_loop(0, BLOCKS, body, 0)


def attend_back(
    head, acts_ref, weights_ref, factor_ref, d_attended_ref, slope_ref, d_logits_ref, d_proj_ref, sums_ref
):
    sums = [None] * BLOCKS
    for pair in range(2):
        upto = (pair + 1) * 256
        pair_rows = pl.ds(pair * 256, 256)
        d_weights = dot_right_t(d_attended_ref[head, pair_rows, :], acts_ref[head, 0:upto, VALUE])
        for i in (2 * pair, 2 * pair + 1):
            at = (i - 2 * pair) * BLOCK
            for j in range(i + 1):
                d_logits = d_weights[at : at + BLOCK, tile_rows(j)] * factor_ref[head, tile_rows(i), tile_rows(j)]
                sums[i - j] = d_logits if sums[i - j] is None else sums[i - j] + d_logits
                d_logits_ref[tile_rows(i), tile_rows(j)] = d_logits.astype(BF16)
        d_query = dot(d_logits_ref[pair_rows, 0:upto], acts_ref[head, 0:upto, KEY])
        d_proj_ref[head, pair_rows, QUERY] = (d_query * SCALE * slope_ref[head, pair_rows, QUERY]).astype(BF16)
    for apart in range(BLOCKS):
        sums_ref[head, apart] = sums[apart]
    for pair in range(2):
        pair_rows = pl.ds(pair * 256, 256)
        below = pl.ds(pair * 256, ROWS - pair * 256)
        d_value = dot_left_t(weights_ref[head, below, pair_rows], d_attended_ref[head, below, :])
        d_proj_ref[head, pair_rows, VALUE] = (d_value * slope_ref[head, pair_rows, VALUE]).astype(BF16)
        d_key = dot_left_t(d_logits_ref[below, pair_rows], acts_ref[head, below, QUERY])
        d_proj_ref[head, pair_rows, KEY] = (d_key * SCALE * slope_ref[head, pair_rows, KEY]).astype(BF16)


def bias_sums(sums_ref, bias_ref):
    lane = lax.broadcasted_iota(jnp.int32, (1, 128), 1)
    bias_ref[...] = jnp.zeros_like(bias_ref)

    def body(head, carry):
        totals = [None] * BUCKETS
        for apart in range(BLOCKS):
            distance, bounds = bucket_bounds(apart)
            for at, (bucket, least) in enumerate(bounds):
                value = sums_ref[head, apart]
                if at > 0:
                    value = jnp.where(distance >= least, value, 0.0)
                if at + 1 < len(bounds):
                    value = jnp.where(distance < bounds[at + 1][1], value, 0.0)
                value = jnp.sum(value, axis=0, keepdims=True)
                totals[bucket] = value if totals[bucket] is None else totals[bucket] + value
        packed = jnp.zeros((1, 128), F32)
        for bucket in range(BUCKETS):
            packed = jnp.where(lane == bucket, jnp.sum(totals[bucket], axis=1, keepdims=True), packed)
        bias_ref[pl.ds(head, 1), :] = packed
        return carry

    lax.fori_loop(0, HEADS, body, 0)


def token_grads(part, d_proj_ref, weight_ref, normed_ref, inverse_ref, upstream_ref, token_grad_ref):
    rows = pl.ds(part * 256, 256)
    d_normed = dot_right_t(d_proj_ref[0, rows, :], head_weight(weight_ref, 0, range(4)))
    for h in range(1, HEADS):
        d_normed = d_normed + dot_right_t(d_proj_ref[h, rows, :], head_weight(weight_ref, h, range(4)))
    normed = normed_ref[rows, :]
    inverse = inverse_ref[rows, 0:1]
    mean = jnp.mean(d_normed, axis=-1, keepdims=True)
    along = jnp.mean(d_normed * normed, axis=-1, keepdims=True)
    back = inverse * (d_normed - mean - normed * along)
    token_grad_ref[rows, :] = (upstream_ref[rows, :].astype(F32) + back).astype(BF16)


def place():
    dp = lax.axis_index("dp")
    return lax.axis_index("rep"), lax.div(dp, 2 * NZ), lax.rem(lax.div(dp, 2), NZ), lax.rem(dp, 2)


def device(x, y, z, core):
    return ((y * NZ + z) * 2 + core, x)


def layer_kernel(
    tokens_hbm, cotangent_hbm, weight_hbm, out_weight_hbm, table_hbm, length_hbm, first_hbm, slot_hbm,
    token_grad_ref, proj_grad_ref, out_grad_ref, bias_grad_ref,
    tokens_ref, own_ref, received_ref, weight_ref, out_weight_ref, table_ref, length_ref, first_ref, slot_ref,
    normed_ref, normed_b_ref, inverse_ref, acts_ref, slope_ref, upstream_ref, d_mixed_ref, weights_ref,
    factor_ref, attended_ref, mixed_ref, d_attended_ref, d_logits_ref, d_proj_ref, bias_tile_ref, sums_ref,
    term, core_in, x_out, x_in, x_sum, y_in, y_sum, z_in,
    out_y_in, out_z_all, out_mine, out_x_all, out_core_in,
    bias_core, bias_x, bias_y, bias_z,
    load_sem, cotangent_sem, core_sem, x_sem, y_send, y_recv, z_sem,
    out_y_sem, out_z_sem, out_y_back_sem, out_x_back_sem, out_core_back_sem,
    bias_core_sem, bias_x_sem, bias_y_sem, bias_z_sem,
):
    x, y, z, core = place()
    other = 1 - core
    dp = lax.axis_index("dp")
    n_dp = 2 * NY * NZ

    def x_peer(k):
        return lax.rem(x + k, NX)

    def y_peer(k):
        return lax.rem(y + k, NY)

    def z_peer(k):
        return lax.rem(z + k, NZ)

    def remote(src, dst, send, recv, target):
        return pltpu.make_async_remote_copy(
            src_ref=src, dst_ref=dst, send_sem=send, recv_sem=recv, device_id=target,
            device_id_type=pl.DeviceIdType.MESH,
        )

    loads = [
        pltpu.make_async_copy(tokens_hbm, tokens_ref, load_sem.at[0]),
        pltpu.make_async_copy(table_hbm, table_ref, load_sem.at[1]),
        pltpu.make_async_copy(length_hbm, length_ref, load_sem.at[2]),
        pltpu.make_async_copy(first_hbm, first_ref, load_sem.at[3]),
        pltpu.make_async_copy(slot_hbm, slot_ref, load_sem.at[4]),
        pltpu.make_async_copy(cotangent_hbm.at[pl.ds(0, ROWS)], own_ref, load_sem.at[5]),
        pltpu.make_async_copy(out_weight_hbm, out_weight_ref, load_sem.at[6]),
    ]
    weight_load = pltpu.make_async_copy(weight_hbm, weight_ref, load_sem.at[7])
    for load in loads[:2] + [weight_load] + loads[2:]:
        load.start()

    barrier = pltpu.get_barrier_semaphore()
    greeted = [device(x, y, z, other)]
    greeted += [device(x_peer(k), y, z, core) for k in range(1, NX)]
    greeted += [device(x, y_peer(k), z, core) for k in range(1, NY)]
    greeted += [device(x, y, z_peer(k), core) for k in range(1, NZ)]
    greeted += [(lax.rem(dp + n_dp + 2 * core - 1, n_dp), x)]
    for target in greeted:
        pl.semaphore_signal(barrier, inc=1, device_id=target, device_id_type=pl.DeviceIdType.MESH)

    clear_upper(weights_ref, d_logits_ref)
    loads[1].wait()
    fill_bias(table_ref, bias_tile_ref)
    loads[0].wait()
    norm_tokens(tokens_ref, normed_ref, normed_b_ref, inverse_ref)

    pl.semaphore_wait(barrier, len(greeted))
    cotangent_copy = remote(
        cotangent_hbm.at[pl.ds(ROWS, 2 * BLOCK)], received_ref, cotangent_sem.at[0], cotangent_sem.at[1],
        (lax.rem(dp + n_dp - 1, n_dp), x),
    )
    cotangent_copy.start()

    for load in loads[2:5]:
        load.wait()

    weight_load.wait()

    def forward(head, carry):
        project(head, normed_b_ref, weight_ref, acts_ref, slope_ref)
        attend(head, acts_ref, bias_tile_ref, length_ref, first_ref, weights_ref, factor_ref, attended_ref)
        return carry

    lax.fori_loop(0, HEADS, forward, 0)

    for load in loads[5:]:
        load.wait()
    cotangent_copy.wait_recv()
    take_upstream(own_ref, received_ref, slot_ref, length_ref, first_ref, upstream_ref)
    mix_back(upstream_ref, out_weight_ref, d_mixed_ref)
    mix(acts_ref, attended_ref, d_mixed_ref, slope_ref, mixed_ref, d_attended_ref, d_proj_ref)

    def put_term(s, value):
        units = value.shape[0] // 128
        term[s, 0:units] = value.astype(BF16).reshape(units, 4, 2, 16, D)

    def units_of(s):
        return pl.ds(0, 4 if s < 2 else 3)

    def core_copy(s):
        return remote(
            term.at[s, units_of(s), :, other], core_in.at[s, units_of(s)], core_sem.at[0, s], core_sem.at[1, s],
            device(x, y, z, other),
        )

    def x_copy(s, k):
        return remote(
            x_out.at[s, x_peer(k), units_of(s)], x_in.at[s, k - 1, units_of(s)], x_sem.at[0, s, k - 1], x_sem.at[1, s, k - 1],
            device(x_peer(k), y, z, core),
        )

    def by_lanes(both):
        return [both[:, k * 128 : (k + 1) * 128] for k in range(NX)]

    def by_columns(both):
        upper = lax.broadcasted_iota(jnp.int32, (8, 128), 0) < 4
        parts = []
        for k in range(NX):
            rows = both[(k // 2) * 8 : (k // 2) * 8 + 8]
            quarters = [rows[:, q * 128 : (q + 1) * 128] for q in range(4)]
            if k % 2 == 0:
                pairs = [jnp.where(upper, quarters[q], pltpu.roll(quarters[q + 1], 4, 0)) for q in (0, 2)]
            else:
                pairs = [jnp.where(upper, pltpu.roll(quarters[q], 4, 0), quarters[q + 1]) for q in (0, 2)]
            parts.append(jnp.concatenate(pairs, axis=0))
        return parts

    def after_core(s):
        core_copy(s).wait_recv()

        def body(g, carry):
            for zz in range(4):
                both = term[s, g, zz, core].astype(F32) + core_in[s, g, zz].astype(F32)
                for k, part in enumerate(by_lanes(both) if s == 0 else by_columns(both)):
                    x_out[s, k, g, zz] = part.astype(BF16)
            return carry

        lax.fori_loop(0, 4 if s < 2 else 3, body, 0)
        for k in (2, 1, 3):
            x_copy(s, k).start()

    def after_x(s):
        for k in range(1, NX):
            x_copy(s, k).wait_recv()
        for g in range(4 if s < 2 else 3):
            total = x_out[s, x, g].astype(F32)
            for k in range(NX - 1):
                total = total + x_in[s, k, g].astype(F32)
            x_sum[s, g] = total.astype(BF16)

    def y_copy(g, h):
        to_y = 2 * g + h // 2
        slot = lax.rem(lax.rem(y - to_y + NY - 1, NY), NY - 1)
        return to_y != y, remote(
            x_sum.at[1, h] if g == 0 else x_sum.at[2 + h, g - 1],
            y_in.at[h % 2, slot],
            y_send.at[g, h],
            y_recv.at[h % 2, slot],
            device(x, to_y, z, core),
        )

    def y_start(units):
        for g, h in units:
            away, copy = y_copy(g, h)
            pl.when(away)(copy.start)

    def add_y(half, own):
        for k in range(NY - 1):
            remote(
                x_sum.at[1, 0], y_in.at[half, k], y_send.at[0, 0], y_recv.at[half, k],
                device(x, y_peer(1), z, core),
            ).wait_recv()
        total = own.astype(F32)
        for k in range(NY - 1):
            total = total + y_in[half, k].astype(F32)
        y_sum[half] = total.astype(BF16)

    def after_y_gate():
        @pl.when(y < 2)
        def _():
            for half in range(2):
                add_y(half, x_sum[1, 2 * y + half])

    def after_y(h):
        @pl.when((y >= 2) & (lax.rem(y, 2) == h // 2))
        def _():
            add_y(h % 2, x_sum[2 + h, lax.div(y, 2) - 1])

    def out_chunk(ref, at_y, *lead):
        return ref.at[(*lead, lax.div(at_y, 2), pl.ds(lax.rem(at_y, 2) * 2, 2))]

    def out_y_copy(k):
        return remote(
            out_chunk(x_sum, y_peer(k), 0), out_y_in.at[k - 1], out_y_sem.at[0, k - 1],
            out_y_sem.at[1, k - 1], device(x, y_peer(k), z, core),
        )

    def out_z_copy(k):
        return remote(
            out_z_all.at[z], out_z_all.at[z], out_z_sem.at[0, k - 1], out_z_sem.at[1, k - 1],
            device(x, y, z_peer(k), core),
        )

    def out_y_back_copy(k):
        return remote(
            out_chunk(out_mine, y), out_chunk(out_mine, y), out_y_back_sem.at[0, k - 1],
            out_y_back_sem.at[1, k - 1], device(x, y_peer(k), z, core),
        )

    def out_x_back_copy(k, steps):
        return remote(
            out_chunk(out_mine, y_peer(steps)), out_chunk(out_x_all, y_peer(steps), x),
            out_x_back_sem.at[0, k - 1, steps], out_x_back_sem.at[1, k - 1, steps],
            device(x_peer(k), y, z, core),
        )

    def out_x_back_start(steps):
        for k in (2, 1, 3):
            out_x_back_copy(k, steps).start()

    out_core_back_copy = remote(
        out_x_all, out_core_in, out_core_back_sem.at[0], out_core_back_sem.at[1], device(x, y, z, other)
    )

    def out_y_start():
        for k in range(1, NY):
            out_y_copy(k).start()

    def out_after_y():
        for k in range(1, NY):
            out_y_copy(k).wait_recv()
        total = out_chunk(x_sum, y, 0)[...].astype(F32)
        for k in range(NY - 1):
            total = total + out_y_in[k].astype(F32)
        out_z_all[z] = total.astype(BF16)
        for k in range(1, NZ):
            out_z_copy(k).start()

    def out_after_z():
        for k in range(1, NZ):
            out_z_copy(k).wait_recv()
        total = out_z_all[0].astype(F32)
        for k in range(1, NZ):
            total = total + out_z_all[k].astype(F32)
        out_chunk(out_mine, y)[...] = total.astype(BF16)
        for k in (4, 3, 5, 2, 6, 1, 7):
            out_y_back_copy(k).start()
        out_x_back_start(0)

    def out_after_y_back():
        for k in (1, 7, 2, 6, 3, 5, 4):
            out_y_back_copy(k).wait_recv()
            out_x_back_start(NY - k)
        out_x_all[x] = out_mine[...]

    def out_after_x_back():
        for k in range(1, NX):
            for steps in range(NY):
                out_x_back_copy(k, steps).wait_recv()
        out_core_back_copy.start()

    def out_finish():
        out_core_back_copy.wait_recv()
        for from_core, gathered in ((core, out_x_all), (other, out_core_in)):
            for g in range(4):
                for zz in range(4):
                    at = pl.multiple_of(g * 128 + zz * 32 + from_core * 16, 16)
                    for k in range(NX):
                        out_grad_ref[pl.ds(at, 16), k * 128 : (k + 1) * 128] = gathered[k, g, zz]

    bias_steps = (
        (bias_core, bias_core_sem, core, 2, lambda k: device(x, y, z, other)),
        (bias_x, bias_x_sem, x, NX, lambda k: device(x_peer(k), y, z, core)),
        (bias_y, bias_y_sem, y, NY, lambda k: device(x, y_peer(k), z, core)),
        (bias_z, bias_z_sem, z, NZ, lambda k: device(x, y, z_peer(k), core)),
    )

    def bias_copies(step):
        buffer, sems, at, count, peer = bias_steps[step]
        return [
            remote(buffer.at[at], buffer.at[at], sems.at[0, k - 1], sems.at[1, k - 1], peer(k))
            for k in range(1, count)
        ]

    def bias_start(step, value):
        bias_steps[step][0][bias_steps[step][2]] = value
        for copy in bias_copies(step):
            copy.start()

    def bias_finish(step):
        for copy in bias_copies(step):
            copy.wait_recv()
        buffer, count = bias_steps[step][0], bias_steps[step][3]
        total = buffer[0]
        for k in range(1, count):
            total = total + buffer[k]
        return total

    gate_units = [(0, h) for h in range(HEADS)]

    def head_units(h):
        return [(g, h) for g in range(1, 4)]

    def back(head):
        attend_back(
            head, acts_ref, weights_ref, factor_ref, d_attended_ref, slope_ref, d_logits_ref, d_proj_ref,
            sums_ref,
        )

    def send_head(head):
        put_term(2 + head, dot_left_t(d_proj_ref[head, :, 128:D], normed_b_ref[...]))
        core_copy(2 + head).start()

    def tokens_part(part):
        token_grads(part, d_proj_ref, weight_ref, normed_ref, inverse_ref, upstream_ref, token_grad_ref)

    def z_copy(k):
        to_z = z_peer(k)
        return remote(
            y_sum.at[lax.div(to_z, 4), lax.rem(to_z, 4)], z_in.at[k - 1], z_sem.at[0, k - 1],
            z_sem.at[1, k - 1], device(x, y, to_z, core),
        )

    put_term(0, dot_left_t(mixed_ref[...], upstream_ref[...]))
    core_copy(0).start()
    d_gate = jnp.concatenate([d_proj_ref[h, :, GATE] for h in range(HEADS)], axis=1)
    put_term(1, dot_left_t(d_gate, normed_b_ref[...]))
    core_copy(1).start()
    after_core(0)
    back(0)
    after_core(1)
    send_head(0)
    back(1)
    after_core(2)
    send_head(1)
    back(2)
    after_core(3)
    after_x(0)
    out_y_start()
    send_head(2)
    back(3)
    after_core(4)
    after_x(1)
    y_start(gate_units)
    send_head(3)
    out_after_y()
    bias_sums(sums_ref, bias_grad_ref)
    bias_start(0, bias_grad_ref[...])
    after_core(5)
    tokens_part(0)
    bias_start(1, bias_finish(0))
    after_x(2)
    y_start(head_units(0))
    after_x(3)
    y_start(head_units(1))
    tokens_part(1)
    out_after_z()
    after_x(4)
    y_start(head_units(2))
    after_x(5)
    y_start(head_units(3))
    bias_start(2, bias_finish(1))
    after_y_gate()
    after_y(0)
    after_y(1)
    out_after_y_back()
    bias_start(3, bias_finish(2))
    after_y(2)
    after_y(3)
    for k in (4, 3, 5, 2, 6, 1, 7):
        z_copy(k).start()
    out_after_x_back()

    cotangent_copy.wait_send()
    for s in range(SETS):
        core_copy(s).wait_send()
        for k in range(1, NX):
            x_copy(s, k).wait_send()
    for h in range(HEADS):
        for g in range(4):
            away, copy = y_copy(g, h)
            pl.when(away)(copy.wait_send)
    for k in range(1, NY):
        out_y_copy(k).wait_send()
        out_y_back_copy(k).wait_send()
    for k in range(1, NZ):
        out_z_copy(k).wait_send()
    for k in range(1, NX):
        for steps in range(NY):
            out_x_back_copy(k, steps).wait_send()
    for step in range(4):
        for copy in bias_copies(step):
            copy.wait_send()

    out_finish()
    bias_grad_ref[...] = bias_finish(3)
    for k in range(1, NZ):
        z_copy(k).wait_recv()
    total = y_sum[lax.div(z, 4), lax.rem(z, 4)].astype(F32)
    for k in range(NZ - 1):
        total = total + z_in[k].astype(F32)
    for q in range(4):
        proj_grad_ref[:, q * 128 : (q + 1) * 128] = total[4 * q : 4 * q + 4]
    for k in range(1, NZ):
        z_copy(k).wait_send()
    out_core_back_copy.wait_send()


DMA = pltpu.SemaphoreType.DMA
ARGUMENT_SCRATCH = [
    pltpu.VMEM((ROWS, D), BF16),
    pltpu.VMEM((ROWS, D), BF16),
    pltpu.VMEM((2 * BLOCK, D), BF16),
    pltpu.VMEM((D, 4 * D), BF16),
    pltpu.VMEM((D, D), BF16),
    pltpu.SMEM((HEADS, BUCKETS), F32),
    pltpu.SMEM((BLOCKS,), jnp.int32),
    pltpu.SMEM((BLOCKS,), jnp.int32),
    pltpu.SMEM((BLOCKS,), jnp.int32),
]
LAYER_SCRATCH = [
    pltpu.VMEM((ROWS, D), F32),
    pltpu.VMEM((ROWS, D), BF16),
    pltpu.VMEM((ROWS, BLOCK), F32),
    pltpu.VMEM((HEADS, ROWS, D), BF16),
    pltpu.VMEM((HEADS, ROWS, D), F32),
    pltpu.VMEM((ROWS, D), BF16),
    pltpu.VMEM((HEADS, ROWS, 128), F32),
    pltpu.VMEM((HEADS, ROWS, ROWS), BF16),
    pltpu.VMEM((HEADS, ROWS, ROWS), F32),
    pltpu.VMEM((HEADS, ROWS, 128), F32),
    pltpu.VMEM((ROWS, D), BF16),
    pltpu.VMEM((HEADS, ROWS, 128), BF16),
    pltpu.VMEM((ROWS, ROWS), BF16),
    pltpu.VMEM((HEADS, ROWS, D), BF16),
    pltpu.VMEM((HEADS, BLOCKS, BLOCK, BLOCK), F32),
    pltpu.VMEM((HEADS, BLOCKS, BLOCK, BLOCK), F32),
]
SUM_SCRATCH = [
    pltpu.VMEM((SETS, 4, 4, 2, 16, D), BF16),
    pltpu.VMEM((SETS, 4, 4, 16, D), BF16),
    pltpu.VMEM((SETS, NX, 4, 4, 16, 128), BF16),
    pltpu.VMEM((SETS, NX - 1, 4, 4, 16, 128), BF16),
    pltpu.VMEM((SETS, 4, 4, 16, 128), BF16),
    pltpu.VMEM((2, NY - 1, 4, 16, 128), BF16),
    pltpu.VMEM((2, 4, 16, 128), BF16),
    pltpu.VMEM((NZ - 1, 16, 128), BF16),
    pltpu.VMEM((NY - 1, 2, 16, 128), BF16),
    pltpu.VMEM((NZ, 2, 16, 128), BF16),
    pltpu.VMEM((4, 4, 16, 128), BF16),
    pltpu.VMEM((NX, 4, 4, 16, 128), BF16),
    pltpu.VMEM((NX, 4, 4, 16, 128), BF16),
    pltpu.VMEM((2, 8, 128), F32),
    pltpu.VMEM((NX, 8, 128), F32),
    pltpu.VMEM((NY, 8, 128), F32),
    pltpu.VMEM((NZ, 8, 128), F32),
]
SEMAPHORES = [
    DMA((8,)),
    DMA((2,)),
    DMA((2, SETS)),
    DMA((2, SETS, NX - 1)),
    DMA((HEADS, 4)),
    DMA((2, NY - 1)),
    DMA((2, NZ - 1)),
    DMA((2, NY - 1)),
    DMA((2, NZ - 1)),
    DMA((2, NY - 1)),
    DMA((2, NX - 1, NY)),
    DMA((2,)),
    DMA((2, 1)),
    DMA((2, NX - 1)),
    DMA((2, NY - 1)),
    DMA((2, NZ - 1)),
]


def finish_kernel(token_ref, proj_ref, out_ref, bias_ref, token_hbm, proj_hbm, out_hbm, small_ref, wide_ref, sems):
    copies = [
        pltpu.make_async_copy(token_ref, token_hbm, sems.at[0]),
        pltpu.make_async_copy(proj_ref, proj_hbm, sems.at[1]),
        pltpu.make_async_copy(wide_ref, out_hbm, sems.at[2]),
    ]
    copies[0].start()
    copies[1].start()
    wide_ref[...] = out_ref[...].astype(F32)
    copies[2].start()
    small_ref[...] = bias_ref[0:HEADS, 0:BUCKETS]
    for copy in copies:
        copy.wait()


def finish(*values):
    vmem = pl.BlockSpec(memory_space=pltpu.VMEM)
    hbm = pl.BlockSpec(memory_space=pltpu.HBM)
    return pl.pallas_call(
        finish_kernel,
        out_shape=(
            jax.ShapeDtypeStruct((ROWS, D), BF16),
            jax.ShapeDtypeStruct((4, D), F32),
            jax.ShapeDtypeStruct((D, D), F32),
            jax.ShapeDtypeStruct((HEADS, BUCKETS), F32),
        ),
        in_specs=[vmem] * 4,
        out_specs=(hbm, hbm, hbm, vmem),
        scratch_shapes=[pltpu.VMEM((D, D), F32), DMA((3,))],
        compiler_params=pltpu.CompilerParams(vmem_limit_bytes=8 * 2**20),
        name="finish",
    )(*values)


def shards(tokens, cotangent, weight, out_weight, table, length, first, slot):
    vmem = pl.BlockSpec(memory_space=pltpu.VMEM)
    token_grad, proj_grad, out_grad, bias_grad = pl.pallas_call(
        layer_kernel,
        out_shape=(
            jax.ShapeDtypeStruct((ROWS, D), BF16),
            jax.ShapeDtypeStruct((4, D), F32),
            jax.ShapeDtypeStruct((D, D), BF16),
            jax.ShapeDtypeStruct((8, 128), F32),
        ),
        in_specs=[pl.BlockSpec(memory_space=pltpu.HBM)] * 8,
        out_specs=(vmem,) * 4,
        scratch_shapes=ARGUMENT_SCRATCH + LAYER_SCRATCH + SUM_SCRATCH + SEMAPHORES,
        compiler_params=pltpu.CompilerParams(
            vmem_limit_bytes=52 * 2**20, collective_id=0, has_side_effects=True
        ),
        name="layer_grads",
    )(*(
        pltpu.with_memory_space_constraint(value, pltpu.HBM)
        for value in (tokens, cotangent, weight, out_weight, table, length, first, slot)
    ))
    token_grad, proj_grad, out_grad, bias_grad = finish(token_grad, proj_grad, out_grad, bias_grad)
    return token_grad, proj_grad.T, out_grad, bias_grad


def solution(mesh):
    split = P(("dp", "rep"))
    return jax.shard_map(
        shards,
        mesh=mesh,
        in_specs=(split, split, P(), P(), P(), split, split, split),
        out_specs=(split, P(None, ("dp", "rep")), P(), P()),
        check_vma=False,
    )
```

```python
import jax
import jax.numpy as jnp
from jax import lax
from jax.experimental import pallas as pl
from jax.experimental.pallas import tpu as pltpu
from jax.sharding import PartitionSpec as P

HEADS = 4
HEAD_DIM = 128
BLOCK = 128
BLOCKS = 4
SLOTS = 6
BUCKETS = 10
NX, NY, NZ = 4, 8, 8
SETS = HEADS + 2
D = 512
ROWS = BLOCKS * BLOCK
EPSILON = 1e-06
SCALE = HEAD_DIM ** (-0.5)
BF16 = jnp.bfloat16
F32 = jnp.float32
GATE, VALUE, QUERY, KEY = (slice(g * 128, (g + 1) * 128) for g in range(4))
BUCKETS_AT = (range(0, 8), range(1, 9), range(8, 10), range(9, 10))


def dot(a, b):
    return lax.dot_general(a, b, (((1,), (0,)), ((), ())), preferred_element_type=F32)


def dot_right_t(a, b):
    return lax.dot_general(a, b, (((1,), (1,)), ((), ())), preferred_element_type=F32)


def dot_left_t(a, b):
    return lax.dot_general(a, b, (((0,), (0,)), ((), ())), preferred_element_type=F32)


def row_sum(parts):
    total = parts[0]
    for part in parts[1:]:
        total = total + part
    return jnp.sum(total, axis=-1, keepdims=True)


def tile_iota(axis):
    return lax.broadcasted_iota(jnp.int32, (BLOCK, BLOCK), axis)


def norm_tokens(tokens_ref, normed_ref, normed_b_ref, inverse_ref):
    for b in range(BLOCKS):
        rows = pl.ds(b * BLOCK, BLOCK)
        x = tokens_ref[rows, :].astype(F32)
        centered = x - jnp.mean(x, axis=-1, keepdims=True)
        inverse = lax.rsqrt(jnp.mean(centered * centered, axis=-1, keepdims=True) + EPSILON)
        normed = centered * inverse
        normed_ref[rows, :] = normed
        normed_b_ref[rows, :] = normed.astype(BF16)
        inverse_ref[rows, :] = jnp.broadcast_to(inverse, (BLOCK, BLOCK))


def head_weight(weight_ref, head, groups):
    parts = [weight_ref[:, pl.ds(g * D + head * 128, 128)] for g in groups]
    return jnp.concatenate(parts, axis=1)


def project(head, normed_b_ref, weight_ref, acts_ref, slope_ref):
    for r in range(2):
        for c in range(2):
            rows, lanes = pl.ds(r * 256, 256), pl.ds(c * 256, 256)
            half = dot(normed_b_ref[rows, :], head_weight(weight_ref, head, (2 * c, 2 * c + 1))) * 0.5
            u = 1.0 + jnp.tanh(half)
            act = half * u
            slope_ref[head, rows, lanes] = 0.5 * (u + act * (2.0 - u))
            acts_ref[head, rows, lanes] = act.astype(BF16)


def take_upstream(own_ref, received_ref, slot_ref, length_ref, first_ref, upstream_ref):
    for b in range(BLOCKS):
        rows = pl.ds(b * BLOCK, BLOCK)
        slot = jnp.full((BLOCK, D), lax.rem(slot_ref[b], SLOTS), jnp.int32)
        value = own_ref[0:BLOCK, :].astype(F32)
        for at in range(1, SLOTS):
            ref, row_at = (own_ref, at * BLOCK) if at < BLOCKS else (received_ref, (at - BLOCKS) * BLOCK)
            value = jnp.where(slot == at, ref[row_at : row_at + BLOCK, :].astype(F32), value)
        limit = length_ref[b] - (b - first_ref[b]) * BLOCK
        row = lax.broadcasted_iota(jnp.int32, (BLOCK, D), 0)
        value = jnp.where(row < limit, value, 0.0)
        upstream_ref[rows, :] = value.astype(BF16)


def mix_back(upstream_ref, out_weight_ref, d_mixed_ref):
    for c in range(2):
        part = dot_right_t(upstream_ref[...], out_weight_ref[c * 256 : (c + 1) * 256, :])
        for k in range(2):
            d_mixed_ref[2 * c + k] = part[:, k * 128 : (k + 1) * 128]


def bucket_bounds(apart):
    distance = tile_iota(0) - tile_iota(1) + apart * BLOCK
    return distance, [(bucket, 0 if bucket == 0 else 2 ** (bucket - 1)) for bucket in BUCKETS_AT[apart]]


def tile_rows(i):
    return slice(i * BLOCK, (i + 1) * BLOCK)


def fill_bias(table_ref, bias_tile_ref):
    def body(head, carry):
        for apart in range(BLOCKS):
            distance, bounds = bucket_bounds(apart)
            tile = jnp.full((BLOCK, BLOCK), table_ref[head, bounds[0][0]] * 0.5, F32)
            for bucket, least in bounds[1:]:
                tile = jnp.where(distance >= least, table_ref[head, bucket] * 0.5, tile)
            bias_tile_ref[head, apart] = tile
        return carry

    lax.fori_loop(0, HEADS, body, 0)


def clear_upper(weights_ref, d_logits_ref):
    zero = jnp.zeros((BLOCK, BLOCK), BF16)
    for i in (0, 2):
        d_logits_ref[tile_rows(i), tile_rows(i + 1)] = zero
        for head in range(HEADS):
            weights_ref[head, tile_rows(i), tile_rows(i + 1)] = zero


def attend(head, acts_ref, bias_tile_ref, length_ref, first_ref, weights_ref, factor_ref, attended_ref):
    row = tile_iota(0)
    causal_row = jnp.where(tile_iota(1) <= row, row, ROWS)
    for pair in range(2):
        upto = (pair + 1) * 256
        pair_rows = pl.ds(pair * 256, 256)
        scores = dot_right_t(acts_ref[head, pair_rows, QUERY], acts_ref[head, 0:upto, KEY])
        for i in (2 * pair, 2 * pair + 1):
            at = (i - 2 * pair) * BLOCK
            for j in range(i + 1):
                limit = jnp.where(
                    first_ref[i] == first_ref[j], length_ref[i] - (i - first_ref[i]) * BLOCK, 0
                )
                half = scores[at : at + BLOCK, tile_rows(j)] * (0.5 * SCALE) + bias_tile_ref[head, i - j]
                kept = (causal_row if i == j else row) < limit
                u = jnp.where(kept, 1.0 + jnp.tanh(half), 0.0)
                weight = half * u
                factor_ref[head, tile_rows(i), tile_rows(j)] = 0.5 * (u + weight * (2.0 - u))
                weights_ref[head, tile_rows(i), tile_rows(j)] = weight.astype(BF16)
        attended_ref[head, pair_rows, :] = dot(
            weights_ref[head, pair_rows, 0:upto], acts_ref[head, 0:upto, VALUE]
        )


def mix(acts_ref, attended_ref, d_mixed_ref, slope_ref, mixed_ref, d_attended_ref, d_proj_ref):
    for b in range(BLOCKS):
        rows = pl.ds(b * BLOCK, BLOCK)
        heads = range(HEADS)
        att = [attended_ref[h, rows, :] for h in heads]
        mean = row_sum(att) * (1.0 / D)
        centered = [a - mean for a in att]
        inverse = lax.rsqrt(row_sum([c * c for c in centered]) * (1.0 / D) + EPSILON)
        normed = [c * inverse for c in centered]
        gate = [acts_ref[h, rows, GATE].astype(F32) for h in heads]
        d_mixed = [d_mixed_ref[h, rows, :] for h in heads]
        g = [d_mixed[h] * gate[h] for h in heads]
        g_mean = row_sum(g) * (1.0 / D)
        g_dot = row_sum([g[h] * normed[h] for h in heads]) * (1.0 / D)
        for h in heads:
            mixed_ref[rows, pl.ds(h * 128, 128)] = (normed[h] * gate[h]).astype(BF16)
            d_attended_ref[h, rows, :] = (inverse * (g[h] - g_mean - normed[h] * g_dot)).astype(BF16)
            d_proj_ref[h, rows, GATE] = (d_mixed[h] * normed[h] * slope_ref[h, rows, GATE]).astype(BF16)


def attend_back(
    head, acts_ref, weights_ref, factor_ref, d_attended_ref, slope_ref, d_logits_ref, d_proj_ref, sums_ref
):
    sums = [None] * BLOCKS
    for pair in range(2):
        upto = (pair + 1) * 256
        pair_rows = pl.ds(pair * 256, 256)
        d_weights = dot_right_t(d_attended_ref[head, pair_rows, :], acts_ref[head, 0:upto, VALUE])
        for i in (2 * pair, 2 * pair + 1):
            at = (i - 2 * pair) * BLOCK
            for j in range(i + 1):
                d_logits = d_weights[at : at + BLOCK, tile_rows(j)] * factor_ref[head, tile_rows(i), tile_rows(j)]
                sums[i - j] = d_logits if sums[i - j] is None else sums[i - j] + d_logits
                d_logits_ref[tile_rows(i), tile_rows(j)] = d_logits.astype(BF16)
        d_query = dot(d_logits_ref[pair_rows, 0:upto], acts_ref[head, 0:upto, KEY])
        d_proj_ref[head, pair_rows, QUERY] = (d_query * SCALE * slope_ref[head, pair_rows, QUERY]).astype(BF16)
    for apart in range(BLOCKS):
        sums_ref[head, apart] = sums[apart]
    for pair in range(2):
        pair_rows = pl.ds(pair * 256, 256)
        below = pl.ds(pair * 256, ROWS - pair * 256)
        d_value = dot_left_t(weights_ref[head, below, pair_rows], d_attended_ref[head, below, :])
        d_proj_ref[head, pair_rows, VALUE] = (d_value * slope_ref[head, pair_rows, VALUE]).astype(BF16)
        d_key = dot_left_t(d_logits_ref[below, pair_rows], acts_ref[head, below, QUERY])
        d_proj_ref[head, pair_rows, KEY] = (d_key * SCALE * slope_ref[head, pair_rows, KEY]).astype(BF16)


def bias_sums(sums_ref, bias_ref):
    lane = lax.broadcasted_iota(jnp.int32, (1, 128), 1)
    bias_ref[...] = jnp.zeros_like(bias_ref)

    for head in range(HEADS):
        totals = [None] * BUCKETS
        for apart in range(BLOCKS):
            distance, bounds = bucket_bounds(apart)
            for at, (bucket, least) in enumerate(bounds):
                value = sums_ref[head, apart]
                if at > 0:
                    value = jnp.where(distance >= least, value, 0.0)
                if at + 1 < len(bounds):
                    value = jnp.where(distance < bounds[at + 1][1], value, 0.0)
                value = jnp.sum(value, axis=0, keepdims=True)
                totals[bucket] = value if totals[bucket] is None else totals[bucket] + value
        packed = jnp.zeros((1, 128), F32)
        for bucket in range(BUCKETS):
            packed = jnp.where(lane == bucket, jnp.sum(totals[bucket], axis=1, keepdims=True), packed)
        bias_ref[pl.ds(head, 1), :] = packed


def token_grads(part, d_proj_ref, weight_ref, normed_ref, inverse_ref, upstream_ref, token_grad_ref):
    rows = pl.ds(part * 256, 256)
    d_normed = dot_right_t(d_proj_ref[0, rows, :], head_weight(weight_ref, 0, range(4)))
    for h in range(1, HEADS):
        d_normed = d_normed + dot_right_t(d_proj_ref[h, rows, :], head_weight(weight_ref, h, range(4)))
    normed = normed_ref[rows, :]
    inverse = inverse_ref[rows, 0:1]
    mean = jnp.mean(d_normed, axis=-1, keepdims=True)
    along = jnp.mean(d_normed * normed, axis=-1, keepdims=True)
    back = inverse * (d_normed - mean - normed * along)
    token_grad_ref[rows, :] = (upstream_ref[rows, :].astype(F32) + back).astype(BF16)


def place():
    dp = lax.axis_index("dp")
    return lax.axis_index("rep"), lax.div(dp, 2 * NZ), lax.rem(lax.div(dp, 2), NZ), lax.rem(dp, 2)


def device(x, y, z, core):
    return ((y * NZ + z) * 2 + core, x)


def layer_kernel(
    tokens_hbm, cotangent_hbm, weight_hbm, out_weight_hbm, table_hbm, length_hbm, first_hbm, slot_hbm,
    token_grad_ref, proj_grad_ref, out_grad_ref, bias_grad_ref,
    tokens_ref, own_ref, received_ref, weight_ref, out_weight_ref, table_ref, length_ref, first_ref, slot_ref,
    normed_ref, normed_b_ref, inverse_ref, acts_ref, slope_ref, upstream_ref, d_mixed_ref, weights_ref,
    factor_ref, attended_ref, mixed_ref, d_attended_ref, d_logits_ref, d_proj_ref, bias_tile_ref, sums_ref,
    term, core_in, x_out, x_in, x_sum, y_in, y_sum, z_in,
    out_y_in, out_z_all, out_mine, out_x_all, out_core_in,
    bias_core, bias_x, bias_y, bias_z,
    load_sem, cotangent_sem, core_sem, x_sem, y_send, y_recv, z_sem,
    out_y_sem, out_z_sem, out_y_back_sem, out_x_back_sem, out_core_back_sem,
    bias_core_sem, bias_x_sem, bias_y_sem, bias_z_sem,
):
    x, y, z, core = place()
    other = 1 - core
    dp = lax.axis_index("dp")
    n_dp = 2 * NY * NZ

    def x_peer(k):
        return lax.rem(x + k, NX)

    def y_peer(k):
        return lax.rem(y + k, NY)

    def z_peer(k):
        return lax.rem(z + k, NZ)

    def remote(src, dst, send, recv, target):
        return pltpu.make_async_remote_copy(
            src_ref=src, dst_ref=dst, send_sem=send, recv_sem=recv, device_id=target,
            device_id_type=pl.DeviceIdType.MESH,
        )

    loads = [
        pltpu.make_async_copy(tokens_hbm, tokens_ref, load_sem.at[0]),
        pltpu.make_async_copy(table_hbm, table_ref, load_sem.at[1]),
        pltpu.make_async_copy(length_hbm, length_ref, load_sem.at[2]),
        pltpu.make_async_copy(first_hbm, first_ref, load_sem.at[3]),
        pltpu.make_async_copy(slot_hbm, slot_ref, load_sem.at[4]),
        pltpu.make_async_copy(cotangent_hbm.at[pl.ds(0, ROWS)], own_ref, load_sem.at[5]),
        pltpu.make_async_copy(out_weight_hbm, out_weight_ref, load_sem.at[6]),
    ]
    weight_load = pltpu.make_async_copy(weight_hbm, weight_ref, load_sem.at[7])
    for load in loads[:2] + [weight_load] + loads[2:]:
        load.start()

    barrier = pltpu.get_barrier_semaphore()
    greeted = [device(x, y, z, other)]
    greeted += [device(x_peer(k), y, z, core) for k in range(1, NX)]
    greeted += [device(x, y_peer(k), z, core) for k in range(1, NY)]
    greeted += [device(x, y, z_peer(k), core) for k in range(1, NZ)]
    greeted += [(lax.rem(dp + n_dp + 2 * core - 1, n_dp), x)]
    for target in greeted:
        pl.semaphore_signal(barrier, inc=1, device_id=target, device_id_type=pl.DeviceIdType.MESH)

    clear_upper(weights_ref, d_logits_ref)
    loads[1].wait()
    fill_bias(table_ref, bias_tile_ref)
    loads[0].wait()
    norm_tokens(tokens_ref, normed_ref, normed_b_ref, inverse_ref)

    pl.semaphore_wait(barrier, len(greeted))
    cotangent_copy = remote(
        cotangent_hbm.at[pl.ds(ROWS, 2 * BLOCK)], received_ref, cotangent_sem.at[0], cotangent_sem.at[1],
        (lax.rem(dp + n_dp - 1, n_dp), x),
    )
    cotangent_copy.start()

    for load in loads[2:5]:
        load.wait()

    weight_load.wait()

    project(0, normed_b_ref, weight_ref, acts_ref, slope_ref)
    for head in range(HEADS):
        if head + 1 < HEADS:
            project(head + 1, normed_b_ref, weight_ref, acts_ref, slope_ref)
        attend(head, acts_ref, bias_tile_ref, length_ref, first_ref, weights_ref, factor_ref, attended_ref)

    for load in loads[5:]:
        load.wait()
    cotangent_copy.wait_recv()
    take_upstream(own_ref, received_ref, slot_ref, length_ref, first_ref, upstream_ref)
    mix_back(upstream_ref, out_weight_ref, d_mixed_ref)
    mix(acts_ref, attended_ref, d_mixed_ref, slope_ref, mixed_ref, d_attended_ref, d_proj_ref)

    def put_term(s, value):
        units = value.shape[0] // 128
        term[s, 0:units] = value.astype(BF16).reshape(units, 4, 2, 16, D)

    def units_of(s):
        return pl.ds(0, 4 if s < 2 else 3)

    def core_copy(s):
        return remote(
            term.at[s, units_of(s), :, other], core_in.at[s, units_of(s)], core_sem.at[0, s], core_sem.at[1, s],
            device(x, y, z, other),
        )

    def x_copy(s, k):
        return remote(
            x_out.at[s, x_peer(k), units_of(s)], x_in.at[s, k - 1, units_of(s)], x_sem.at[0, s, k - 1], x_sem.at[1, s, k - 1],
            device(x_peer(k), y, z, core),
        )

    def by_lanes(both):
        return [both[:, k * 128 : (k + 1) * 128] for k in range(NX)]

    def by_columns(both):
        upper = lax.broadcasted_iota(jnp.int32, (8, 128), 0) < 4
        parts = []
        for k in range(NX):
            rows = both[(k // 2) * 8 : (k // 2) * 8 + 8]
            quarters = [rows[:, q * 128 : (q + 1) * 128] for q in range(4)]
            if k % 2 == 0:
                pairs = [jnp.where(upper, quarters[q], pltpu.roll(quarters[q + 1], 4, 0)) for q in (0, 2)]
            else:
                pairs = [jnp.where(upper, pltpu.roll(quarters[q], 4, 0), quarters[q + 1]) for q in (0, 2)]
            parts.append(jnp.concatenate(pairs, axis=0))
        return parts

    def after_core(s):
        core_copy(s).wait_recv()

        def body(g, carry):
            for zz in range(4):
                both = term[s, g, zz, core].astype(F32) + core_in[s, g, zz].astype(F32)
                for k, part in enumerate(by_lanes(both) if s == 0 else by_columns(both)):
                    x_out[s, k, g, zz] = part.astype(BF16)
            return carry

        lax.fori_loop(0, 4 if s < 2 else 3, body, 0)
        for k in (2, 1, 3):
            x_copy(s, k).start()

    def after_x(s):
        for k in range(1, NX):
            x_copy(s, k).wait_recv()
        for g in range(4 if s < 2 else 3):
            total = x_out[s, x, g].astype(F32)
            for k in range(NX - 1):
                total = total + x_in[s, k, g].astype(F32)
            x_sum[s, g] = total.astype(BF16)

    def y_copy(g, h):
        to_y = 2 * g + h // 2
        slot = lax.rem(lax.rem(y - to_y + NY - 1, NY), NY - 1)
        return to_y != y, remote(
            x_sum.at[1, h] if g == 0 else x_sum.at[2 + h, g - 1],
            y_in.at[h % 2, slot],
            y_send.at[g, h],
            y_recv.at[h % 2, slot],
            device(x, to_y, z, core),
        )

    def y_start(units):
        for g, h in units:
            away, copy = y_copy(g, h)
            pl.when(away)(copy.start)

    def add_y(half, own):
        for k in range(NY - 1):
            remote(
                x_sum.at[1, 0], y_in.at[half, k], y_send.at[0, 0], y_recv.at[half, k],
                device(x, y_peer(1), z, core),
            ).wait_recv()
        total = own.astype(F32)
        for k in range(NY - 1):
            total = total + y_in[half, k].astype(F32)
        y_sum[half] = total.astype(BF16)

    def after_y_gate():
        @pl.when(y < 2)
        def _():
            for half in range(2):
                add_y(half, x_sum[1, 2 * y + half])

    def after_y(h):
        @pl.when((y >= 2) & (lax.rem(y, 2) == h // 2))
        def _():
            add_y(h % 2, x_sum[2 + h, lax.div(y, 2) - 1])

    def out_chunk(ref, at_y, *lead):
        return ref.at[(*lead, lax.div(at_y, 2), pl.ds(lax.rem(at_y, 2) * 2, 2))]

    def out_y_copy(k):
        return remote(
            out_chunk(x_sum, y_peer(k), 0), out_y_in.at[k - 1], out_y_sem.at[0, k - 1],
            out_y_sem.at[1, k - 1], device(x, y_peer(k), z, core),
        )

    def out_z_copy(k):
        return remote(
            out_z_all.at[z], out_z_all.at[z], out_z_sem.at[0, k - 1], out_z_sem.at[1, k - 1],
            device(x, y, z_peer(k), core),
        )

    def out_y_back_copy(k):
        return remote(
            out_chunk(out_mine, y), out_chunk(out_mine, y), out_y_back_sem.at[0, k - 1],
            out_y_back_sem.at[1, k - 1], device(x, y_peer(k), z, core),
        )

    def out_x_back_copy(k, steps):
        return remote(
            out_chunk(out_mine, y_peer(steps)), out_chunk(out_x_all, y_peer(steps), x),
            out_x_back_sem.at[0, k - 1, steps], out_x_back_sem.at[1, k - 1, steps],
            device(x_peer(k), y, z, core),
        )

    def out_x_back_start(steps):
        for k in (2, 1, 3):
            out_x_back_copy(k, steps).start()

    out_core_back_copy = remote(
        out_x_all, out_core_in, out_core_back_sem.at[0], out_core_back_sem.at[1], device(x, y, z, other)
    )

    def out_y_start():
        for k in range(1, NY):
            out_y_copy(k).start()

    def out_after_y():
        for k in range(1, NY):
            out_y_copy(k).wait_recv()
        total = out_chunk(x_sum, y, 0)[...].astype(F32)
        for k in range(NY - 1):
            total = total + out_y_in[k].astype(F32)
        out_z_all[z] = total.astype(BF16)
        for k in range(1, NZ):
            out_z_copy(k).start()

    def out_after_z():
        for k in range(1, NZ):
            out_z_copy(k).wait_recv()
        total = out_z_all[0].astype(F32)
        for k in range(1, NZ):
            total = total + out_z_all[k].astype(F32)
        out_chunk(out_mine, y)[...] = total.astype(BF16)
        for k in (4, 3, 5, 2, 6, 1, 7):
            out_y_back_copy(k).start()
        out_x_back_start(0)

    def out_after_y_back():
        for k in (1, 7, 2, 6, 3, 5, 4):
            out_y_back_copy(k).wait_recv()
            out_x_back_start(NY - k)
        out_x_all[x] = out_mine[...]

    def out_after_x_back():
        for k in range(1, NX):
            for steps in range(NY):
                out_x_back_copy(k, steps).wait_recv()
        out_core_back_copy.start()

    def out_finish():
        out_core_back_copy.wait_recv()
        for from_core, gathered in ((core, out_x_all), (other, out_core_in)):
            for g in range(4):
                for zz in range(4):
                    at = pl.multiple_of(g * 128 + zz * 32 + from_core * 16, 16)
                    for k in range(NX):
                        out_grad_ref[pl.ds(at, 16), k * 128 : (k + 1) * 128] = gathered[k, g, zz]

    bias_steps = (
        (bias_core, bias_core_sem, core, 2, lambda k: device(x, y, z, other)),
        (bias_x, bias_x_sem, x, NX, lambda k: device(x_peer(k), y, z, core)),
        (bias_y, bias_y_sem, y, NY, lambda k: device(x, y_peer(k), z, core)),
        (bias_z, bias_z_sem, z, NZ, lambda k: device(x, y, z_peer(k), core)),
    )

    def bias_copies(step):
        buffer, sems, at, count, peer = bias_steps[step]
        return [
            remote(buffer.at[at], buffer.at[at], sems.at[0, k - 1], sems.at[1, k - 1], peer(k))
            for k in range(1, count)
        ]

    def bias_start(step, value):
        bias_steps[step][0][bias_steps[step][2]] = value
        for copy in bias_copies(step):
            copy.start()

    def bias_finish(step):
        for copy in bias_copies(step):
            copy.wait_recv()
        buffer, count = bias_steps[step][0], bias_steps[step][3]
        total = buffer[0]
        for k in range(1, count):
            total = total + buffer[k]
        return total

    gate_units = [(0, h) for h in range(HEADS)]

    def head_units(h):
        return [(g, h) for g in range(1, 4)]

    def back(head):
        attend_back(
            head, acts_ref, weights_ref, factor_ref, d_attended_ref, slope_ref, d_logits_ref, d_proj_ref,
            sums_ref,
        )

    def send_head(head):
        put_term(2 + head, dot_left_t(d_proj_ref[head, :, 128:D], normed_b_ref[...]))
        core_copy(2 + head).start()

    def tokens_part(part):
        token_grads(part, d_proj_ref, weight_ref, normed_ref, inverse_ref, upstream_ref, token_grad_ref)

    def z_copy(k):
        to_z = z_peer(k)
        return remote(
            y_sum.at[lax.div(to_z, 4), lax.rem(to_z, 4)], z_in.at[k - 1], z_sem.at[0, k - 1],
            z_sem.at[1, k - 1], device(x, y, to_z, core),
        )

    put_term(0, dot_left_t(mixed_ref[...], upstream_ref[...]))
    core_copy(0).start()
    d_gate = jnp.concatenate([d_proj_ref[h, :, GATE] for h in range(HEADS)], axis=1)
    put_term(1, dot_left_t(d_gate, normed_b_ref[...]))
    core_copy(1).start()
    after_core(0)
    back(0)
    after_core(1)
    send_head(0)
    back(1)
    after_core(2)
    send_head(1)
    back(2)
    after_core(3)
    after_x(0)
    out_y_start()
    send_head(2)
    back(3)
    after_core(4)
    after_x(1)
    y_start(gate_units)
    send_head(3)
    out_after_y()
    bias_sums(sums_ref, bias_grad_ref)
    bias_start(0, bias_grad_ref[...])
    after_core(5)
    tokens_part(0)
    bias_start(1, bias_finish(0))
    after_x(2)
    y_start(head_units(0))
    after_x(3)
    y_start(head_units(1))
    tokens_part(1)
    out_after_z()
    after_x(4)
    y_start(head_units(2))
    after_x(5)
    y_start(head_units(3))
    bias_start(2, bias_finish(1))
    after_y_gate()
    after_y(0)
    after_y(1)
    out_after_y_back()
    bias_start(3, bias_finish(2))
    after_y(2)
    after_y(3)
    for k in (4, 3, 5, 2, 6, 1, 7):
        z_copy(k).start()
    out_after_x_back()

    cotangent_copy.wait_send()
    for s in range(SETS):
        core_copy(s).wait_send()
        for k in range(1, NX):
            x_copy(s, k).wait_send()
    for h in range(HEADS):
        for g in range(4):
            away, copy = y_copy(g, h)
            pl.when(away)(copy.wait_send)
    for k in range(1, NY):
        out_y_copy(k).wait_send()
        out_y_back_copy(k).wait_send()
    for k in range(1, NZ):
        out_z_copy(k).wait_send()
    for k in range(1, NX):
        for steps in range(NY):
            out_x_back_copy(k, steps).wait_send()
    for step in range(4):
        for copy in bias_copies(step):
            copy.wait_send()

    out_finish()
    bias_grad_ref[...] = bias_finish(3)
    for k in range(1, NZ):
        z_copy(k).wait_recv()
    total = y_sum[lax.div(z, 4), lax.rem(z, 4)].astype(F32)
    for k in range(NZ - 1):
        total = total + z_in[k].astype(F32)
    for q in range(4):
        proj_grad_ref[:, q * 128 : (q + 1) * 128] = total[4 * q : 4 * q + 4]
    for k in range(1, NZ):
        z_copy(k).wait_send()
    out_core_back_copy.wait_send()


DMA = pltpu.SemaphoreType.DMA
ARGUMENT_SCRATCH = [
    pltpu.VMEM((ROWS, D), BF16),
    pltpu.VMEM((ROWS, D), BF16),
    pltpu.VMEM((2 * BLOCK, D), BF16),
    pltpu.VMEM((D, 4 * D), BF16),
    pltpu.VMEM((D, D), BF16),
    pltpu.SMEM((HEADS, BUCKETS), F32),
    pltpu.SMEM((BLOCKS,), jnp.int32),
    pltpu.SMEM((BLOCKS,), jnp.int32),
    pltpu.SMEM((BLOCKS,), jnp.int32),
]
LAYER_SCRATCH = [
    pltpu.VMEM((ROWS, D), F32),
    pltpu.VMEM((ROWS, D), BF16),
    pltpu.VMEM((ROWS, BLOCK), F32),
    pltpu.VMEM((HEADS, ROWS, D), BF16),
    pltpu.VMEM((HEADS, ROWS, D), F32),
    pltpu.VMEM((ROWS, D), BF16),
    pltpu.VMEM((HEADS, ROWS, 128), F32),
    pltpu.VMEM((HEADS, ROWS, ROWS), BF16),
    pltpu.VMEM((HEADS, ROWS, ROWS), F32),
    pltpu.VMEM((HEADS, ROWS, 128), F32),
    pltpu.VMEM((ROWS, D), BF16),
    pltpu.VMEM((HEADS, ROWS, 128), BF16),
    pltpu.VMEM((ROWS, ROWS), BF16),
    pltpu.VMEM((HEADS, ROWS, D), BF16),
    pltpu.VMEM((HEADS, BLOCKS, BLOCK, BLOCK), F32),
    pltpu.VMEM((HEADS, BLOCKS, BLOCK, BLOCK), F32),
]
SUM_SCRATCH = [
    pltpu.VMEM((SETS, 4, 4, 2, 16, D), BF16),
    pltpu.VMEM((SETS, 4, 4, 16, D), BF16),
    pltpu.VMEM((SETS, NX, 4, 4, 16, 128), BF16),
    pltpu.VMEM((SETS, NX - 1, 4, 4, 16, 128), BF16),
    pltpu.VMEM((SETS, 4, 4, 16, 128), BF16),
    pltpu.VMEM((2, NY - 1, 4, 16, 128), BF16),
    pltpu.VMEM((2, 4, 16, 128), BF16),
    pltpu.VMEM((NZ - 1, 16, 128), BF16),
    pltpu.VMEM((NY - 1, 2, 16, 128), BF16),
    pltpu.VMEM((NZ, 2, 16, 128), BF16),
    pltpu.VMEM((4, 4, 16, 128), BF16),
    pltpu.VMEM((NX, 4, 4, 16, 128), BF16),
    pltpu.VMEM((NX, 4, 4, 16, 128), BF16),
    pltpu.VMEM((2, 8, 128), F32),
    pltpu.VMEM((NX, 8, 128), F32),
    pltpu.VMEM((NY, 8, 128), F32),
    pltpu.VMEM((NZ, 8, 128), F32),
]
SEMAPHORES = [
    DMA((8,)),
    DMA((2,)),
    DMA((2, SETS)),
    DMA((2, SETS, NX - 1)),
    DMA((HEADS, 4)),
    DMA((2, NY - 1)),
    DMA((2, NZ - 1)),
    DMA((2, NY - 1)),
    DMA((2, NZ - 1)),
    DMA((2, NY - 1)),
    DMA((2, NX - 1, NY)),
    DMA((2,)),
    DMA((2, 1)),
    DMA((2, NX - 1)),
    DMA((2, NY - 1)),
    DMA((2, NZ - 1)),
]


def finish_kernel(token_ref, proj_ref, out_ref, bias_ref, token_hbm, proj_hbm, out_hbm, small_ref, wide_ref, sems):
    copies = [
        pltpu.make_async_copy(token_ref, token_hbm, sems.at[0]),
        pltpu.make_async_copy(proj_ref, proj_hbm, sems.at[1]),
        pltpu.make_async_copy(wide_ref, out_hbm, sems.at[2]),
    ]
    copies[0].start()
    copies[1].start()
    wide_ref[...] = out_ref[...].astype(F32)
    copies[2].start()
    small_ref[...] = bias_ref[0:HEADS, 0:BUCKETS]
    for copy in copies:
        copy.wait()


def finish(*values):
    vmem = pl.BlockSpec(memory_space=pltpu.VMEM)
    hbm = pl.BlockSpec(memory_space=pltpu.HBM)
    return pl.pallas_call(
        finish_kernel,
        out_shape=(
            jax.ShapeDtypeStruct((ROWS, D), BF16),
            jax.ShapeDtypeStruct((4, D), F32),
            jax.ShapeDtypeStruct((D, D), F32),
            jax.ShapeDtypeStruct((HEADS, BUCKETS), F32),
        ),
        in_specs=[vmem] * 4,
        out_specs=(hbm, hbm, hbm, vmem),
        scratch_shapes=[pltpu.VMEM((D, D), F32), DMA((3,))],
        compiler_params=pltpu.CompilerParams(vmem_limit_bytes=8 * 2**20),
        name="finish",
    )(*values)


def shards(tokens, cotangent, weight, out_weight, table, length, first, slot):
    vmem = pl.BlockSpec(memory_space=pltpu.VMEM)
    token_grad, proj_grad, out_grad, bias_grad = pl.pallas_call(
        layer_kernel,
        out_shape=(
            jax.ShapeDtypeStruct((ROWS, D), BF16),
            jax.ShapeDtypeStruct((4, D), F32),
            jax.ShapeDtypeStruct((D, D), BF16),
            jax.ShapeDtypeStruct((8, 128), F32),
        ),
        in_specs=[pl.BlockSpec(memory_space=pltpu.HBM)] * 8,
        out_specs=(vmem,) * 4,
        scratch_shapes=ARGUMENT_SCRATCH + LAYER_SCRATCH + SUM_SCRATCH + SEMAPHORES,
        compiler_params=pltpu.CompilerParams(
            vmem_limit_bytes=52 * 2**20, collective_id=0, has_side_effects=True
        ),
        name="layer_grads",
    )(*(
        pltpu.with_memory_space_constraint(value, pltpu.HBM)
        for value in (tokens, cotangent, weight, out_weight, table, length, first, slot)
    ))
    token_grad, proj_grad, out_grad, bias_grad = finish(token_grad, proj_grad, out_grad, bias_grad)
    return token_grad, proj_grad.T, out_grad, bias_grad


def solution(mesh):
    split = P(("dp", "rep"))
    return jax.shard_map(
        shards,
        mesh=mesh,
        in_specs=(split, split, P(), P(), P(), split, split, split),
        out_specs=(split, P(None, ("dp", "rep")), P(), P()),
        check_vma=False,
    )
```

```python
import jax
import jax.numpy as jnp
from jax import lax
from jax.experimental import pallas as pl
from jax.experimental.pallas import tpu as pltpu
from jax.sharding import PartitionSpec as P

HEADS = 4
HEAD_DIM = 128
BLOCK = 128
BLOCKS = 4
SLOTS = 6
BUCKETS = 10
NX, NY, NZ = 4, 8, 8
SETS = HEADS + 2
D = 512
ROWS = BLOCKS * BLOCK
EPSILON = 1e-06
SCALE = HEAD_DIM ** (-0.5)
BF16 = jnp.bfloat16
F32 = jnp.float32
GATE, VALUE, QUERY, KEY = (slice(g * 128, (g + 1) * 128) for g in range(4))
BUCKETS_AT = (range(0, 8), range(1, 9), range(8, 10), range(9, 10))


def dot(a, b):
    return lax.dot_general(a, b, (((1,), (0,)), ((), ())), preferred_element_type=F32)


def dot_right_t(a, b):
    return lax.dot_general(a, b, (((1,), (1,)), ((), ())), preferred_element_type=F32)


def dot_left_t(a, b):
    return lax.dot_general(a, b, (((0,), (0,)), ((), ())), preferred_element_type=F32)


def row_sum(parts):
    total = parts[0]
    for part in parts[1:]:
        total = total + part
    return jnp.sum(total, axis=-1, keepdims=True)


def tile_iota(axis):
    return lax.broadcasted_iota(jnp.int32, (BLOCK, BLOCK), axis)


def norm_tokens(tokens_ref, normed_ref, normed_b_ref, inverse_ref):
    for b in range(BLOCKS):
        rows = pl.ds(b * BLOCK, BLOCK)
        x = tokens_ref[rows, :].astype(F32)
        centered = x - jnp.mean(x, axis=-1, keepdims=True)
        inverse = lax.rsqrt(jnp.mean(centered * centered, axis=-1, keepdims=True) + EPSILON)
        normed = centered * inverse
        normed_ref[rows, :] = normed
        normed_b_ref[rows, :] = normed.astype(BF16)
        inverse_ref[rows, :] = jnp.broadcast_to(inverse, (BLOCK, BLOCK))


def head_weight(weight_ref, head, groups):
    parts = [weight_ref[:, pl.ds(g * D + head * 128, 128)] for g in groups]
    return jnp.concatenate(parts, axis=1)


def project(head, normed_b_ref, weight_ref, acts_ref, slope_ref):
    for r in range(2):
        for c in range(2):
            rows, lanes = pl.ds(r * 256, 256), pl.ds(c * 256, 256)
            half = dot(normed_b_ref[rows, :], head_weight(weight_ref, head, (2 * c, 2 * c + 1))) * 0.5
            u = 1.0 + jnp.tanh(half)
            act = half * u
            slope_ref[head, rows, lanes] = 0.5 * (u + act * (2.0 - u))
            acts_ref[head, rows, lanes] = act.astype(BF16)


def take_upstream(own_ref, received_ref, slot_ref, length_ref, first_ref, upstream_ref):
    for b in range(BLOCKS):
        rows = pl.ds(b * BLOCK, BLOCK)
        slot = jnp.full((BLOCK, D), lax.rem(slot_ref[b], SLOTS), jnp.int32)
        value = own_ref[0:BLOCK, :].astype(F32)
        for at in range(1, SLOTS):
            ref, row_at = (own_ref, at * BLOCK) if at < BLOCKS else (received_ref, (at - BLOCKS) * BLOCK)
            value = jnp.where(slot == at, ref[row_at : row_at + BLOCK, :].astype(F32), value)
        limit = length_ref[b] - (b - first_ref[b]) * BLOCK
        row = lax.broadcasted_iota(jnp.int32, (BLOCK, D), 0)
        value = jnp.where(row < limit, value, 0.0)
        upstream_ref[rows, :] = value.astype(BF16)


def mix_back(upstream_ref, out_weight_ref, d_mixed_ref):
    for c in range(2):
        part = dot_right_t(upstream_ref[...], out_weight_ref[c * 256 : (c + 1) * 256, :])
        for k in range(2):
            d_mixed_ref[2 * c + k] = part[:, k * 128 : (k + 1) * 128]


def bucket_bounds(apart):
    distance = tile_iota(0) - tile_iota(1) + apart * BLOCK
    return distance, [(bucket, 0 if bucket == 0 else 2 ** (bucket - 1)) for bucket in BUCKETS_AT[apart]]


def tile_rows(i):
    return slice(i * BLOCK, (i + 1) * BLOCK)


def fill_bias(table_ref, bias_tile_ref):
    def body(head, carry):
        for apart in range(BLOCKS):
            distance, bounds = bucket_bounds(apart)
            tile = jnp.full((BLOCK, BLOCK), table_ref[head, bounds[0][0]] * 0.5, F32)
            for bucket, least in bounds[1:]:
                tile = jnp.where(distance >= least, table_ref[head, bucket] * 0.5, tile)
            bias_tile_ref[head, apart] = tile
        return carry

    lax.fori_loop(0, HEADS, body, 0)


def clear_upper(weights_ref, d_logits_ref):
    zero = jnp.zeros((BLOCK, BLOCK), BF16)
    for i in (0, 2):
        d_logits_ref[tile_rows(i), tile_rows(i + 1)] = zero
        for head in range(HEADS):
            weights_ref[head, tile_rows(i), tile_rows(i + 1)] = zero


def attend(head, acts_ref, bias_tile_ref, length_ref, first_ref, weights_ref, factor_ref, attended_ref):
    row = tile_iota(0)
    causal_row = jnp.where(tile_iota(1) <= row, row, ROWS)
    for pair in range(2):
        upto = (pair + 1) * 256
        pair_rows = pl.ds(pair * 256, 256)
        scores = dot_right_t(acts_ref[head, pair_rows, QUERY], acts_ref[head, 0:upto, KEY])
        for i in (2 * pair, 2 * pair + 1):
            at = (i - 2 * pair) * BLOCK
            for j in range(i + 1):
                limit = jnp.where(
                    first_ref[i] == first_ref[j], length_ref[i] - (i - first_ref[i]) * BLOCK, 0
                )
                half = scores[at : at + BLOCK, tile_rows(j)] * (0.5 * SCALE) + bias_tile_ref[head, i - j]
                kept = (causal_row if i == j else row) < limit
                u = jnp.where(kept, 1.0 + jnp.tanh(half), 0.0)
                weight = half * u
                factor_ref[head, tile_rows(i), tile_rows(j)] = 0.5 * (u + weight * (2.0 - u))
                weights_ref[head, tile_rows(i), tile_rows(j)] = weight.astype(BF16)
        attended_ref[head, pair_rows, :] = dot(
            weights_ref[head, pair_rows, 0:upto], acts_ref[head, 0:upto, VALUE]
        )


def mix(acts_ref, attended_ref, att_inverse_ref, mixed_ref):
    heads = range(HEADS)
    for b in range(BLOCKS):
        rows = pl.ds(b * BLOCK, BLOCK)
        att = [attended_ref[h, rows, :] for h in heads]
        mean = row_sum(att) * (1.0 / D)
        centered = [a - mean for a in att]
        inverse = lax.rsqrt(row_sum([c * c for c in centered]) * (1.0 / D) + EPSILON)
        att_inverse_ref[rows, :] = jnp.broadcast_to(inverse, (BLOCK, BLOCK))
        for h in heads:
            normed = centered[h] * inverse
            attended_ref[h, rows, :] = normed
            mixed_ref[rows, pl.ds(h * 128, 128)] = (normed * acts_ref[h, rows, GATE].astype(F32)).astype(BF16)


def mix_grads(acts_ref, attended_ref, att_inverse_ref, d_mixed_ref, slope_ref, d_attended_ref, d_proj_ref):
    heads = range(HEADS)
    for b in range(BLOCKS):
        rows = pl.ds(b * BLOCK, BLOCK)
        normed = [attended_ref[h, rows, :] for h in heads]
        inverse = att_inverse_ref[rows, 0:1]
        d_mixed = [d_mixed_ref[h, rows, :] for h in heads]
        g = [d_mixed[h] * acts_ref[h, rows, GATE].astype(F32) for h in heads]
        g_mean = row_sum(g) * (1.0 / D)
        g_dot = row_sum([g[h] * normed[h] for h in heads]) * (1.0 / D)
        for h in heads:
            d_attended_ref[h, rows, :] = (inverse * (g[h] - g_mean - normed[h] * g_dot)).astype(BF16)
            d_proj_ref[h, rows, GATE] = (d_mixed[h] * normed[h] * slope_ref[h, rows, GATE]).astype(BF16)


def attend_back(
    head, acts_ref, weights_ref, factor_ref, d_attended_ref, slope_ref, d_logits_ref, d_proj_ref, sums_ref
):
    sums = [None] * BLOCKS
    for pair in range(2):
        upto = (pair + 1) * 256
        pair_rows = pl.ds(pair * 256, 256)
        d_weights = dot_right_t(d_attended_ref[head, pair_rows, :], acts_ref[head, 0:upto, VALUE])
        for i in (2 * pair, 2 * pair + 1):
            at = (i - 2 * pair) * BLOCK
            for j in range(i + 1):
                d_logits = d_weights[at : at + BLOCK, tile_rows(j)] * factor_ref[head, tile_rows(i), tile_rows(j)]
                sums[i - j] = d_logits if sums[i - j] is None else sums[i - j] + d_logits
                d_logits_ref[tile_rows(i), tile_rows(j)] = d_logits.astype(BF16)
        d_query = dot(d_logits_ref[pair_rows, 0:upto], acts_ref[head, 0:upto, KEY])
        d_proj_ref[head, pair_rows, QUERY] = (d_query * SCALE * slope_ref[head, pair_rows, QUERY]).astype(BF16)
    for apart in range(BLOCKS):
        sums_ref[head, apart] = sums[apart]
    for pair in range(2):
        pair_rows = pl.ds(pair * 256, 256)
        below = pl.ds(pair * 256, ROWS - pair * 256)
        d_value = dot_left_t(weights_ref[head, below, pair_rows], d_attended_ref[head, below, :])
        d_proj_ref[head, pair_rows, VALUE] = (d_value * slope_ref[head, pair_rows, VALUE]).astype(BF16)
        d_key = dot_left_t(d_logits_ref[below, pair_rows], acts_ref[head, below, QUERY])
        d_proj_ref[head, pair_rows, KEY] = (d_key * SCALE * slope_ref[head, pair_rows, KEY]).astype(BF16)


def bias_sums(sums_ref, bias_ref):
    lane = lax.broadcasted_iota(jnp.int32, (1, 128), 1)
    bias_ref[...] = jnp.zeros_like(bias_ref)

    for head in range(HEADS):
        totals = [None] * BUCKETS
        for apart in range(BLOCKS):
            distance, bounds = bucket_bounds(apart)
            for at, (bucket, least) in enumerate(bounds):
                value = sums_ref[head, apart]
                if at > 0:
                    value = jnp.where(distance >= least, value, 0.0)
                if at + 1 < len(bounds):
                    value = jnp.where(distance < bounds[at + 1][1], value, 0.0)
                value = jnp.sum(value, axis=0, keepdims=True)
                totals[bucket] = value if totals[bucket] is None else totals[bucket] + value
        packed = jnp.zeros((1, 128), F32)
        for bucket in range(BUCKETS):
            packed = jnp.where(lane == bucket, jnp.sum(totals[bucket], axis=1, keepdims=True), packed)
        bias_ref[pl.ds(head, 1), :] = packed


def token_grads(part, d_proj_ref, weight_ref, normed_ref, inverse_ref, upstream_ref, token_grad_ref):
    rows = pl.ds(part * 256, 256)
    d_normed = dot_right_t(d_proj_ref[0, rows, :], head_weight(weight_ref, 0, range(4)))
    for h in range(1, HEADS):
        d_normed = d_normed + dot_right_t(d_proj_ref[h, rows, :], head_weight(weight_ref, h, range(4)))
    normed = normed_ref[rows, :]
    inverse = inverse_ref[rows, 0:1]
    mean = jnp.mean(d_normed, axis=-1, keepdims=True)
    along = jnp.mean(d_normed * normed, axis=-1, keepdims=True)
    back = inverse * (d_normed - mean - normed * along)
    token_grad_ref[rows, :] = (upstream_ref[rows, :].astype(F32) + back).astype(BF16)


def place():
    dp = lax.axis_index("dp")
    return lax.axis_index("rep"), lax.div(dp, 2 * NZ), lax.rem(lax.div(dp, 2), NZ), lax.rem(dp, 2)


def device(x, y, z, core):
    return ((y * NZ + z) * 2 + core, x)


def layer_kernel(
    tokens_hbm, cotangent_hbm, weight_hbm, out_weight_hbm, table_hbm, length_hbm, first_hbm, slot_hbm,
    token_grad_ref, proj_grad_ref, out_grad_ref, bias_grad_ref,
    tokens_ref, own_ref, received_ref, weight_ref, out_weight_ref, table_ref, length_ref, first_ref, slot_ref,
    normed_ref, normed_b_ref, inverse_ref, acts_ref, slope_ref, upstream_ref, d_mixed_ref, weights_ref,
    factor_ref, attended_ref, mixed_ref, d_attended_ref, d_logits_ref, d_proj_ref, bias_tile_ref, sums_ref, att_inverse_ref,
    term, core_in, x_out, x_in, x_sum, y_in, y_sum, z_in,
    out_y_in, out_z_all, out_mine, out_x_all, out_core_in,
    bias_core, bias_x, bias_y, bias_z,
    load_sem, cotangent_sem, core_sem, x_sem, y_send, y_recv, z_sem,
    out_y_sem, out_z_sem, out_y_back_sem, out_x_back_sem, out_core_back_sem,
    bias_core_sem, bias_x_sem, bias_y_sem, bias_z_sem,
):
    x, y, z, core = place()
    other = 1 - core
    dp = lax.axis_index("dp")
    n_dp = 2 * NY * NZ

    def x_peer(k):
        return lax.rem(x + k, NX)

    def y_peer(k):
        return lax.rem(y + k, NY)

    def z_peer(k):
        return lax.rem(z + k, NZ)

    def remote(src, dst, send, recv, target):
        return pltpu.make_async_remote_copy(
            src_ref=src, dst_ref=dst, send_sem=send, recv_sem=recv, device_id=target,
            device_id_type=pl.DeviceIdType.MESH,
        )

    loads = [
        pltpu.make_async_copy(tokens_hbm, tokens_ref, load_sem.at[0]),
        pltpu.make_async_copy(table_hbm, table_ref, load_sem.at[1]),
        pltpu.make_async_copy(length_hbm, length_ref, load_sem.at[2]),
        pltpu.make_async_copy(first_hbm, first_ref, load_sem.at[3]),
        pltpu.make_async_copy(slot_hbm, slot_ref, load_sem.at[4]),
        pltpu.make_async_copy(cotangent_hbm.at[pl.ds(0, ROWS)], own_ref, load_sem.at[5]),
        pltpu.make_async_copy(out_weight_hbm, out_weight_ref, load_sem.at[6]),
    ]
    weight_load = pltpu.make_async_copy(weight_hbm, weight_ref, load_sem.at[7])
    for load in loads[:2] + [weight_load] + loads[2:]:
        load.start()

    barrier = pltpu.get_barrier_semaphore()
    greeted = [device(x, y, z, other)]
    greeted += [device(x_peer(k), y, z, core) for k in range(1, NX)]
    greeted += [device(x, y_peer(k), z, core) for k in range(1, NY)]
    greeted += [device(x, y, z_peer(k), core) for k in range(1, NZ)]
    greeted += [(lax.rem(dp + n_dp + 2 * core - 1, n_dp), x)]
    for target in greeted:
        pl.semaphore_signal(barrier, inc=1, device_id=target, device_id_type=pl.DeviceIdType.MESH)

    clear_upper(weights_ref, d_logits_ref)
    loads[1].wait()
    fill_bias(table_ref, bias_tile_ref)
    loads[0].wait()
    norm_tokens(tokens_ref, normed_ref, normed_b_ref, inverse_ref)

    pl.semaphore_wait(barrier, len(greeted))
    cotangent_copy = remote(
        cotangent_hbm.at[pl.ds(ROWS, 2 * BLOCK)], received_ref, cotangent_sem.at[0], cotangent_sem.at[1],
        (lax.rem(dp + n_dp - 1, n_dp), x),
    )
    cotangent_copy.start()

    for load in loads[2:5]:
        load.wait()

    weight_load.wait()

    project(0, normed_b_ref, weight_ref, acts_ref, slope_ref)
    for head in range(HEADS):
        if head + 1 < HEADS:
            project(head + 1, normed_b_ref, weight_ref, acts_ref, slope_ref)
        attend(head, acts_ref, bias_tile_ref, length_ref, first_ref, weights_ref, factor_ref, attended_ref)

    for load in loads[5:]:
        load.wait()
    cotangent_copy.wait_recv()
    take_upstream(own_ref, received_ref, slot_ref, length_ref, first_ref, upstream_ref)
    mix(acts_ref, attended_ref, att_inverse_ref, mixed_ref)

    def put_term(s, value):
        units = value.shape[0] // 128
        term[s, 0:units] = value.astype(BF16).reshape(units, 4, 2, 16, D)

    def units_of(s):
        return pl.ds(0, 4 if s < 2 else 3)

    def core_copy(s):
        return remote(
            term.at[s, units_of(s), :, other], core_in.at[s, units_of(s)], core_sem.at[0, s], core_sem.at[1, s],
            device(x, y, z, other),
        )

    def x_copy(s, k):
        return remote(
            x_out.at[s, x_peer(k), units_of(s)], x_in.at[s, k - 1, units_of(s)], x_sem.at[0, s, k - 1], x_sem.at[1, s, k - 1],
            device(x_peer(k), y, z, core),
        )

    def by_lanes(both):
        return [both[:, k * 128 : (k + 1) * 128] for k in range(NX)]

    def by_columns(both):
        upper = lax.broadcasted_iota(jnp.int32, (8, 128), 0) < 4
        parts = []
        for k in range(NX):
            rows = both[(k // 2) * 8 : (k // 2) * 8 + 8]
            quarters = [rows[:, q * 128 : (q + 1) * 128] for q in range(4)]
            if k % 2 == 0:
                pairs = [jnp.where(upper, quarters[q], pltpu.roll(quarters[q + 1], 4, 0)) for q in (0, 2)]
            else:
                pairs = [jnp.where(upper, pltpu.roll(quarters[q], 4, 0), quarters[q + 1]) for q in (0, 2)]
            parts.append(jnp.concatenate(pairs, axis=0))
        return parts

    def after_core(s):
        core_copy(s).wait_recv()

        def body(g, carry):
            for zz in range(4):
                both = term[s, g, zz, core].astype(F32) + core_in[s, g, zz].astype(F32)
                for k, part in enumerate(by_lanes(both) if s == 0 else by_columns(both)):
                    x_out[s, k, g, zz] = part.astype(BF16)
            return carry

        lax.fori_loop(0, 4 if s < 2 else 3, body, 0)
        for k in (2, 1, 3):
            x_copy(s, k).start()

    def after_x(s):
        for k in range(1, NX):
            x_copy(s, k).wait_recv()
        for g in range(4 if s < 2 else 3):
            total = x_out[s, x, g].astype(F32)
            for k in range(NX - 1):
                total = total + x_in[s, k, g].astype(F32)
            x_sum[s, g] = total.astype(BF16)

    def y_copy(g, h):
        to_y = 2 * g + h // 2
        slot = lax.rem(lax.rem(y - to_y + NY - 1, NY), NY - 1)
        return to_y != y, remote(
            x_sum.at[1, h] if g == 0 else x_sum.at[2 + h, g - 1],
            y_in.at[h % 2, slot],
            y_send.at[g, h],
            y_recv.at[h % 2, slot],
            device(x, to_y, z, core),
        )

    def y_start(units):
        for g, h in units:
            away, copy = y_copy(g, h)
            pl.when(away)(copy.start)

    def add_y(half, own):
        for k in range(NY - 1):
            remote(
                x_sum.at[1, 0], y_in.at[half, k], y_send.at[0, 0], y_recv.at[half, k],
                device(x, y_peer(1), z, core),
            ).wait_recv()
        total = own.astype(F32)
        for k in range(NY - 1):
            total = total + y_in[half, k].astype(F32)
        y_sum[half] = total.astype(BF16)

    def after_y_gate():
        @pl.when(y < 2)
        def _():
            for half in range(2):
                add_y(half, x_sum[1, 2 * y + half])

    def after_y(h):
        @pl.when((y >= 2) & (lax.rem(y, 2) == h // 2))
        def _():
            add_y(h % 2, x_sum[2 + h, lax.div(y, 2) - 1])

    def out_chunk(ref, at_y, *lead):
        return ref.at[(*lead, lax.div(at_y, 2), pl.ds(lax.rem(at_y, 2) * 2, 2))]

    def out_y_copy(k):
        return remote(
            out_chunk(x_sum, y_peer(k), 0), out_y_in.at[k - 1], out_y_sem.at[0, k - 1],
            out_y_sem.at[1, k - 1], device(x, y_peer(k), z, core),
        )

    def out_z_copy(k):
        return remote(
            out_z_all.at[z], out_z_all.at[z], out_z_sem.at[0, k - 1], out_z_sem.at[1, k - 1],
            device(x, y, z_peer(k), core),
        )

    def out_y_back_copy(k):
        return remote(
            out_chunk(out_mine, y), out_chunk(out_mine, y), out_y_back_sem.at[0, k - 1],
            out_y_back_sem.at[1, k - 1], device(x, y_peer(k), z, core),
        )

    def out_x_back_copy(k, steps):
        return remote(
            out_chunk(out_mine, y_peer(steps)), out_chunk(out_x_all, y_peer(steps), x),
            out_x_back_sem.at[0, k - 1, steps], out_x_back_sem.at[1, k - 1, steps],
            device(x_peer(k), y, z, core),
        )

    def out_x_back_start(steps):
        for k in (2, 1, 3):
            out_x_back_copy(k, steps).start()

    out_core_back_copy = remote(
        out_x_all, out_core_in, out_core_back_sem.at[0], out_core_back_sem.at[1], device(x, y, z, other)
    )

    def out_y_start():
        for k in range(1, NY):
            out_y_copy(k).start()

    def out_after_y():
        for k in range(1, NY):
            out_y_copy(k).wait_recv()
        total = out_chunk(x_sum, y, 0)[...].astype(F32)
        for k in range(NY - 1):
            total = total + out_y_in[k].astype(F32)
        out_z_all[z] = total.astype(BF16)
        for k in range(1, NZ):
            out_z_copy(k).start()

    def out_after_z():
        for k in range(1, NZ):
            out_z_copy(k).wait_recv()
        total = out_z_all[0].astype(F32)
        for k in range(1, NZ):
            total = total + out_z_all[k].astype(F32)
        out_chunk(out_mine, y)[...] = total.astype(BF16)
        for k in (4, 3, 5, 2, 6, 1, 7):
            out_y_back_copy(k).start()
        out_x_back_start(0)

    def out_after_y_back():
        for k in (1, 7, 2, 6, 3, 5, 4):
            out_y_back_copy(k).wait_recv()
            out_x_back_start(NY - k)
        out_x_all[x] = out_mine[...]

    def out_after_x_back():
        for k in range(1, NX):
            for steps in range(NY):
                out_x_back_copy(k, steps).wait_recv()
        out_core_back_copy.start()

    def out_finish():
        out_core_back_copy.wait_recv()
        for from_core, gathered in ((core, out_x_all), (other, out_core_in)):
            for g in range(4):
                for zz in range(4):
                    at = pl.multiple_of(g * 128 + zz * 32 + from_core * 16, 16)
                    for k in range(NX):
                        out_grad_ref[pl.ds(at, 16), k * 128 : (k + 1) * 128] = gathered[k, g, zz]

    bias_steps = (
        (bias_core, bias_core_sem, core, 2, lambda k: device(x, y, z, other)),
        (bias_x, bias_x_sem, x, NX, lambda k: device(x_peer(k), y, z, core)),
        (bias_y, bias_y_sem, y, NY, lambda k: device(x, y_peer(k), z, core)),
        (bias_z, bias_z_sem, z, NZ, lambda k: device(x, y, z_peer(k), core)),
    )

    def bias_copies(step):
        buffer, sems, at, count, peer = bias_steps[step]
        return [
            remote(buffer.at[at], buffer.at[at], sems.at[0, k - 1], sems.at[1, k - 1], peer(k))
            for k in range(1, count)
        ]

    def bias_start(step, value):
        bias_steps[step][0][bias_steps[step][2]] = value
        for copy in bias_copies(step):
            copy.start()

    def bias_finish(step):
        for copy in bias_copies(step):
            copy.wait_recv()
        buffer, count = bias_steps[step][0], bias_steps[step][3]
        total = buffer[0]
        for k in range(1, count):
            total = total + buffer[k]
        return total

    gate_units = [(0, h) for h in range(HEADS)]

    def head_units(h):
        return [(g, h) for g in range(1, 4)]

    def back(head):
        attend_back(
            head, acts_ref, weights_ref, factor_ref, d_attended_ref, slope_ref, d_logits_ref, d_proj_ref,
            sums_ref,
        )

    def send_head(head):
        put_term(2 + head, dot_left_t(d_proj_ref[head, :, 128:D], normed_b_ref[...]))
        core_copy(2 + head).start()

    def tokens_part(part):
        token_grads(part, d_proj_ref, weight_ref, normed_ref, inverse_ref, upstream_ref, token_grad_ref)

    def z_copy(k):
        to_z = z_peer(k)
        return remote(
            y_sum.at[lax.div(to_z, 4), lax.rem(to_z, 4)], z_in.at[k - 1], z_sem.at[0, k - 1],
            z_sem.at[1, k - 1], device(x, y, to_z, core),
        )

    put_term(0, dot_left_t(mixed_ref[...], upstream_ref[...]))
    core_copy(0).start()
    mix_back(upstream_ref, out_weight_ref, d_mixed_ref)
    mix_grads(acts_ref, attended_ref, att_inverse_ref, d_mixed_ref, slope_ref, d_attended_ref, d_proj_ref)
    d_gate = jnp.concatenate([d_proj_ref[h, :, GATE] for h in range(HEADS)], axis=1)
    put_term(1, dot_left_t(d_gate, normed_b_ref[...]))
    core_copy(1).start()
    after_core(0)
    back(0)
    after_core(1)
    send_head(0)
    back(1)
    after_core(2)
    send_head(1)
    back(2)
    after_core(3)
    after_x(0)
    out_y_start()
    send_head(2)
    back(3)
    after_core(4)
    after_x(1)
    y_start(gate_units)
    send_head(3)
    out_after_y()
    bias_sums(sums_ref, bias_grad_ref)
    bias_start(0, bias_grad_ref[...])
    after_core(5)
    tokens_part(0)
    bias_start(1, bias_finish(0))
    after_x(2)
    y_start(head_units(0))
    after_x(3)
    y_start(head_units(1))
    tokens_part(1)
    out_after_z()
    after_x(4)
    y_start(head_units(2))
    after_x(5)
    y_start(head_units(3))
    bias_start(2, bias_finish(1))
    after_y_gate()
    after_y(0)
    after_y(1)
    out_after_y_back()
    bias_start(3, bias_finish(2))
    after_y(2)
    after_y(3)
    for k in (4, 3, 5, 2, 6, 1, 7):
        z_copy(k).start()
    out_after_x_back()

    cotangent_copy.wait_send()
    for s in range(SETS):
        core_copy(s).wait_send()
        for k in range(1, NX):
            x_copy(s, k).wait_send()
    for h in range(HEADS):
        for g in range(4):
            away, copy = y_copy(g, h)
            pl.when(away)(copy.wait_send)
    for k in range(1, NY):
        out_y_copy(k).wait_send()
        out_y_back_copy(k).wait_send()
    for k in range(1, NZ):
        out_z_copy(k).wait_send()
    for k in range(1, NX):
        for steps in range(NY):
            out_x_back_copy(k, steps).wait_send()
    for step in range(4):
        for copy in bias_copies(step):
            copy.wait_send()

    out_finish()
    bias_grad_ref[...] = bias_finish(3)
    for k in range(1, NZ):
        z_copy(k).wait_recv()
    total = y_sum[lax.div(z, 4), lax.rem(z, 4)].astype(F32)
    for k in range(NZ - 1):
        total = total + z_in[k].astype(F32)
    for q in range(4):
        proj_grad_ref[:, q * 128 : (q + 1) * 128] = total[4 * q : 4 * q + 4]
    for k in range(1, NZ):
        z_copy(k).wait_send()
    out_core_back_copy.wait_send()


DMA = pltpu.SemaphoreType.DMA
ARGUMENT_SCRATCH = [
    pltpu.VMEM((ROWS, D), BF16),
    pltpu.VMEM((ROWS, D), BF16),
    pltpu.VMEM((2 * BLOCK, D), BF16),
    pltpu.VMEM((D, 4 * D), BF16),
    pltpu.VMEM((D, D), BF16),
    pltpu.SMEM((HEADS, BUCKETS), F32),
    pltpu.SMEM((BLOCKS,), jnp.int32),
    pltpu.SMEM((BLOCKS,), jnp.int32),
    pltpu.SMEM((BLOCKS,), jnp.int32),
]
LAYER_SCRATCH = [
    pltpu.VMEM((ROWS, D), F32),
    pltpu.VMEM((ROWS, D), BF16),
    pltpu.VMEM((ROWS, BLOCK), F32),
    pltpu.VMEM((HEADS, ROWS, D), BF16),
    pltpu.VMEM((HEADS, ROWS, D), F32),
    pltpu.VMEM((ROWS, D), BF16),
    pltpu.VMEM((HEADS, ROWS, 128), F32),
    pltpu.VMEM((HEADS, ROWS, ROWS), BF16),
    pltpu.VMEM((HEADS, ROWS, ROWS), F32),
    pltpu.VMEM((HEADS, ROWS, 128), F32),
    pltpu.VMEM((ROWS, D), BF16),
    pltpu.VMEM((HEADS, ROWS, 128), BF16),
    pltpu.VMEM((ROWS, ROWS), BF16),
    pltpu.VMEM((HEADS, ROWS, D), BF16),
    pltpu.VMEM((HEADS, BLOCKS, BLOCK, BLOCK), F32),
    pltpu.VMEM((HEADS, BLOCKS, BLOCK, BLOCK), F32),
    pltpu.VMEM((ROWS, BLOCK), F32),
]
SUM_SCRATCH = [
    pltpu.VMEM((SETS, 4, 4, 2, 16, D), BF16),
    pltpu.VMEM((SETS, 4, 4, 16, D), BF16),
    pltpu.VMEM((SETS, NX, 4, 4, 16, 128), BF16),
    pltpu.VMEM((SETS, NX - 1, 4, 4, 16, 128), BF16),
    pltpu.VMEM((SETS, 4, 4, 16, 128), BF16),
    pltpu.VMEM((2, NY - 1, 4, 16, 128), BF16),
    pltpu.VMEM((2, 4, 16, 128), BF16),
    pltpu.VMEM((NZ - 1, 16, 128), BF16),
    pltpu.VMEM((NY - 1, 2, 16, 128), BF16),
    pltpu.VMEM((NZ, 2, 16, 128), BF16),
    pltpu.VMEM((4, 4, 16, 128), BF16),
    pltpu.VMEM((NX, 4, 4, 16, 128), BF16),
    pltpu.VMEM((NX, 4, 4, 16, 128), BF16),
    pltpu.VMEM((2, 8, 128), F32),
    pltpu.VMEM((NX, 8, 128), F32),
    pltpu.VMEM((NY, 8, 128), F32),
    pltpu.VMEM((NZ, 8, 128), F32),
]
SEMAPHORES = [
    DMA((8,)),
    DMA((2,)),
    DMA((2, SETS)),
    DMA((2, SETS, NX - 1)),
    DMA((HEADS, 4)),
    DMA((2, NY - 1)),
    DMA((2, NZ - 1)),
    DMA((2, NY - 1)),
    DMA((2, NZ - 1)),
    DMA((2, NY - 1)),
    DMA((2, NX - 1, NY)),
    DMA((2,)),
    DMA((2, 1)),
    DMA((2, NX - 1)),
    DMA((2, NY - 1)),
    DMA((2, NZ - 1)),
]


def finish_kernel(token_ref, proj_ref, out_ref, bias_ref, token_hbm, proj_hbm, out_hbm, small_ref, wide_ref, sems):
    copies = [
        pltpu.make_async_copy(token_ref, token_hbm, sems.at[0]),
        pltpu.make_async_copy(proj_ref, proj_hbm, sems.at[1]),
        pltpu.make_async_copy(wide_ref, out_hbm, sems.at[2]),
    ]
    copies[0].start()
    copies[1].start()
    wide_ref[...] = out_ref[...].astype(F32)
    copies[2].start()
    small_ref[...] = bias_ref[0:HEADS, 0:BUCKETS]
    for copy in copies:
        copy.wait()


def finish(*values):
    vmem = pl.BlockSpec(memory_space=pltpu.VMEM)
    hbm = pl.BlockSpec(memory_space=pltpu.HBM)
    return pl.pallas_call(
        finish_kernel,
        out_shape=(
            jax.ShapeDtypeStruct((ROWS, D), BF16),
            jax.ShapeDtypeStruct((4, D), F32),
            jax.ShapeDtypeStruct((D, D), F32),
            jax.ShapeDtypeStruct((HEADS, BUCKETS), F32),
        ),
        in_specs=[vmem] * 4,
        out_specs=(hbm, hbm, hbm, vmem),
        scratch_shapes=[pltpu.VMEM((D, D), F32), DMA((3,))],
        compiler_params=pltpu.CompilerParams(vmem_limit_bytes=8 * 2**20),
        name="finish",
    )(*values)


def shards(tokens, cotangent, weight, out_weight, table, length, first, slot):
    vmem = pl.BlockSpec(memory_space=pltpu.VMEM)
    token_grad, proj_grad, out_grad, bias_grad = pl.pallas_call(
        layer_kernel,
        out_shape=(
            jax.ShapeDtypeStruct((ROWS, D), BF16),
            jax.ShapeDtypeStruct((4, D), F32),
            jax.ShapeDtypeStruct((D, D), BF16),
            jax.ShapeDtypeStruct((8, 128), F32),
        ),
        in_specs=[pl.BlockSpec(memory_space=pltpu.HBM)] * 8,
        out_specs=(vmem,) * 4,
        scratch_shapes=ARGUMENT_SCRATCH + LAYER_SCRATCH + SUM_SCRATCH + SEMAPHORES,
        compiler_params=pltpu.CompilerParams(
            vmem_limit_bytes=52 * 2**20, collective_id=0, has_side_effects=True
        ),
        name="layer_grads",
    )(*(
        pltpu.with_memory_space_constraint(value, pltpu.HBM)
        for value in (tokens, cotangent, weight, out_weight, table, length, first, slot)
    ))
    token_grad, proj_grad, out_grad, bias_grad = finish(token_grad, proj_grad, out_grad, bias_grad)
    return token_grad, proj_grad.T, out_grad, bias_grad


def solution(mesh):
    split = P(("dp", "rep"))
    return jax.shard_map(
        shards,
        mesh=mesh,
        in_specs=(split, split, P(), P(), P(), split, split, split),
        out_specs=(split, P(None, ("dp", "rep")), P(), P()),
        check_vma=False,
    )
```
